32 devices in a mesh: section: 4 (over x, core), tp: 2 (over y), doc: 4 (over z).
Axes of the slice: x: 2, y: 2, z: 4, core: 2. Of those that a mesh axis runs over, the one named last changes fastest.
Arguments:
- token_ids: int32 [8, 2, 32], P('doc'), may hold values from 0 to 16383
- seg_lengths: int32 [8, 2], P('doc'), may hold values from 1 to 32
- emb_table: bfloat16 [16384, 4096], P('section', 'tp'), may hold values from -6 to 6
- mem_init: bfloat16 [16, 4096], P(None, 'tp'), may hold values from -6 to 6
- norm_gain: float32 [4, 4096], P('section'), may hold values from 0.1 to 1.9
- w_query: bfloat16 [4, 4096, 2048], P('section', 'doc', 'tp'), may hold values from -0.09375 to 0.09375
- w_key: bfloat16 [4, 4096, 2048], P('section', 'doc', 'tp'), may hold values from -0.09375 to 0.09375
- w_value: bfloat16 [4, 4096, 2048], P('section', 'doc', 'tp'), may hold values from -0.09375 to 0.09375
- w_out: bfloat16 [4, 2048, 4096], P('section', None, 'tp'), may hold values from -0.125 to 0.125
- layer_mix: float32 [4], P('section'), may hold values from 0.5 to 4.5
Outputs:
- pooled: float32 [8, 4096], P(None, 'tp')
The draws below stay inside these ranges and needn't reach their ends.
All inputs are finite; a program needn't handle non-finite values.
Results may differ from the reference program's by a relative error of at most 0.013.
Values may be sent and summed in bfloat16 or wider, within the bound.
No kernel may reach another device: no remote copies, remote signals or barrier semaphores. Data moves between devices by JAX's collectives and lax.ppermute only.
A program may use at most 192 MiB of HBM per device.

```python
import math
import jax
import jax.numpy as jnp
import numpy as np
from jax import lax

D = 4096
HD = 128
HEADS = 16
VOCAB = 16384
M = 16
L = 32
SEGS = 2
SECTIONS = 4
DOCS = 8


def draw_layer_mix(key, part):
    position = jnp.arange(SECTIONS).astype(jnp.float32)
    rising = 1.0 + 2.0 * position / max(SECTIONS - 1, 1)
    factor = jax.random.uniform(jax.random.fold_in(key, 31), (SECTIONS,), jnp.float32, 0.7, 1.3)
    return (rising * factor).astype(jnp.float32)


def set_ends(values, stream_key, low, largest):
    extent = values.shape
    index_at = [jax.random.randint(jax.random.fold_in(stream_key, axis), (), 0, extent[axis]) for axis in range(len(extent))]
    values = values.at[tuple(index_at)].set(low)
    longest = extent.index(max(extent))
    index_at[longest] = (index_at[longest] + 1) % extent[longest]
    return values.at[tuple(index_at)].set(largest)


def levels(own_key, dims, split, low, largest):
    factor_of = 1.0
    for dim, blocks in split:
        heights = jax.random.uniform(jax.random.fold_in(jax.random.fold_in(own_key, 6), dim), (blocks,), jnp.float32, low / len(split), largest / len(split))
        factor_of = factor_of * jnp.repeat(jnp.exp(heights), dims[dim] // blocks).reshape((-1,) + (1,) * (len(dims) - 1 - dim))
    return factor_of


def rank_bounds(number_of, slope):
    portions = [(1 << 20) // math.isqrt(rank ** slope) + 1 for rank in range(1, number_of + 1)]
    scale = 1 + sum(portions) // (1 << 30)
    return np.cumsum(np.array([max(1, weight // scale) for weight in portions]))


def ranked(stream_key, extent, number_of, slope):
    table = rank_bounds(number_of, slope)
    lot = jax.random.randint(jax.random.fold_in(stream_key, 1), extent, 0, int(table[number_of - 1]))
    grade = jnp.searchsorted(jnp.asarray(table, jnp.int32), lot, side="right")
    return jax.random.permutation(jax.random.fold_in(stream_key, 2), number_of)[grade].astype(jnp.int32)


def normal_values(rng, extent, spread, most, cuts=(), held_as=jnp.bfloat16):
    array = jax.random.normal(rng, extent, jnp.float32) * spread
    if len(cuts) > 0:
        array = levels(rng, extent, cuts, -0.22, 0.18) * array
    return jnp.clip(array, min=-most, max=most).astype(held_as)


def setup_inputs(seed: int = 0) -> dict:
    key_of = jax.random.split(jax.random.key(seed), 11)
    token_ids = set_ends(ranked(key_of[0], (DOCS, SEGS, L), VOCAB, 2), jax.random.fold_in(key_of[0], 3), 0, VOCAB - 1).astype(jnp.int32)
    seg_lengths = set_ends(jax.random.randint(key_of[1], (DOCS, SEGS), 1, L + 1), jax.random.fold_in(key_of[1], 1), 1, L).astype(jnp.int32)
    emb_table = normal_values(key_of[2], (VOCAB, D), 1.0, 6.0, ((0, 4), (1, 2)))
    mem_init = normal_values(key_of[3], (M, D), 1.0, 6.0, ((1, 2),))
    norm_gain = jnp.clip(1.0 + 0.18 * jax.random.normal(key_of[4], (SECTIONS, D), jnp.float32), 0.1, 1.9)
    w_query = normal_values(key_of[5], (SECTIONS, D, HEADS * HD), D ** -0.5, 0.09375, ((0, 4), (1, 4), (2, 2)))
    w_key = normal_values(key_of[6], (SECTIONS, D, HEADS * HD), D ** -0.5, 0.09375, ((0, 4), (1, 4), (2, 2)))
    w_value = normal_values(key_of[7], (SECTIONS, D, HEADS * HD), D ** -0.5, 0.09375, ((0, 4), (1, 4), (2, 2)))
    w_out = normal_values(key_of[8], (SECTIONS, HEADS * HD, D), (HEADS * HD) ** -0.5, 0.125, ((0, 4), (2, 2)))
    layer_mix = draw_layer_mix(jax.random.fold_in(key_of[10], 71), 0)
    return dict(token_ids=token_ids, seg_lengths=seg_lengths, emb_table=emb_table, mem_init=mem_init, norm_gain=norm_gain, w_query=w_query, w_key=w_key, w_value=w_value, w_out=w_out, layer_mix=layer_mix)


EPSILON = 1e-05
NEGATIVE = -1e+30

def visible_mask(row_count, lengths):
    position = jnp.arange(row_count)
    key_ok = (position[None, :] < M) | (position[None, :] - M < lengths[:, None])
    ordered = (position[None, :] < M) | (position[:, None] < M) | (position[None, :] <= position[:, None])
    return key_ok[:, None, None, :] & ordered[None, None, :, :]

def layer_apply(hidden, lengths, query_proj, key_proj, value_proj, out_proj, norm_row):
    doc_count, row_count, width = hidden.shape
    floats = hidden.astype(jnp.float32)
    mean_square = lax.optimization_barrier(jnp.mean(floats * floats, -1, keepdims=True))
    normed = (floats * lax.rsqrt(mean_square + EPSILON) * norm_row).astype(jnp.bfloat16)
    normed_wide = normed.astype(jnp.float32)
    queries = jnp.einsum('brd,dk->brk', normed_wide, query_proj.astype(jnp.float32)).astype(jnp.bfloat16)
    keys = jnp.einsum('brd,dk->brk', normed_wide, key_proj.astype(jnp.float32)).astype(jnp.bfloat16)
    values = jnp.einsum('brd,dk->brk', normed_wide, value_proj.astype(jnp.float32)).astype(jnp.bfloat16)
    head_shape = (doc_count, row_count, HEADS, HD)
    scores = jnp.einsum('bqhe,bkhe->bhqk', queries.reshape(head_shape).astype(jnp.float32), keys.reshape(head_shape).astype(jnp.float32)) * (1.0 / math.sqrt(HD))
    allowed = visible_mask(row_count, lengths)
    scores = jnp.where(allowed, scores, NEGATIVE)
    weights = jnp.where(allowed, jnp.exp(scores), 0.0)
    probs = (weights / lax.optimization_barrier(jnp.sum(weights, -1, keepdims=True))).astype(jnp.bfloat16)
    mixed = jnp.einsum('bhqk,bkhe->bqhe', probs.astype(jnp.float32), values.reshape(head_shape).astype(jnp.float32)).astype(jnp.bfloat16)
    update = jnp.einsum('brk,kd->brd', mixed.reshape(doc_count, row_count, HEADS * HD).astype(jnp.float32), out_proj.astype(jnp.float32))
    return (floats + update).astype(jnp.bfloat16)

def reference(token_ids, seg_lengths, emb_table, mem_init, norm_gain, w_query, w_key, w_value, w_out, layer_mix):
    embedded = jnp.take(emb_table, token_ids, axis=0)
    doc_count = token_ids.shape[0]
    memory = jnp.broadcast_to(mem_init, (doc_count, M, mem_init.shape[1]))
    position = jnp.arange(L)
    pooled_layers = None
    for segment in range(SEGS):
        hidden = jnp.concatenate([memory, embedded[:, segment]], 1)
        lengths = seg_lengths[:, segment]
        token_ok = position[None, :] < lengths[:, None]

        def layer_step(carried, params):
            query_proj, key_proj, value_proj, out_proj, norm_row, mixing = params
            result = layer_apply(carried, lengths, query_proj, key_proj, value_proj, out_proj, norm_row)
            summed = lax.optimization_barrier(jnp.sum(jnp.where(token_ok[:, :, None], result[:, M:].astype(jnp.float32), 0.0), 1))
            return (result, mixing * summed / lengths[:, None].astype(jnp.float32))
        hidden, pooled_layers = lax.scan(layer_step, hidden, (w_query, w_key, w_value, w_out, norm_gain, layer_mix))
        memory = hidden[:, :M]
    return lax.optimization_barrier(jnp.sum(pooled_layers, 0))
```

```python
import functools
import math

import jax
import jax.numpy as jnp
from jax import lax
from jax.experimental import pallas as pl
from jax.experimental.pallas import tpu as pltpu
from jax.sharding import PartitionSpec as P

HD = 128
M = 16
EPSILON = 1e-05
AXES = ("section", "tp", "doc")
VMEM_LIMIT = 48 * 1024 * 1024
C_FIRST, C_INIT, C_TP, C_POOL, C_LEN = 0, 1, 2, 3, 4


def attend_kernel(
    turn, docs, tokens, blocks, meta, where, *refs
):
    halves = refs[0]
    other = refs[1]
    tok, tok_other, mem, mem_other, gain = refs[2:7]
    weights = refs[7 : 7 + blocks]
    mixed_ref, keep_ref = refs[7 + blocks : 9 + blocks]
    normed, acc, wbuf, sems = refs[9 + blocks :]
    rows = M + tokens
    half = halves.shape[1]
    depth = wbuf.shape[1]
    cols = wbuf.shape[2] // 3
    copies = []
    for b in range(blocks):
        copy = pltpu.make_async_copy(weights[b], wbuf.at[b], sems.at[b])
        copy.start()
        copies.append(copy)
    first = meta[turn, C_FIRST] == 1
    initial = meta[turn, C_INIT] == 1
    tp = meta[turn, C_TP]

    def prepare(doc, _):
        base = pl.multiple_of(doc * rows, 16)
        tbase = pl.multiple_of(doc * tokens, 16)
        parts = []
        for block, tk, mm in ((halves, tok, mem), (other, tok_other, mem_other)):
            head = jnp.where(initial, mm[...], block[pl.ds(base, M), :])
            body = jnp.where(
                first, tk[pl.ds(tbase, tokens), :], block[pl.ds(base + M, tokens), :]
            )
            parts.append(jnp.concatenate([head, body], 0))
        keep_ref[pl.ds(base, rows), :] = parts[0]
        floats = [p.astype(jnp.float32) for p in parts]
        square = sum(jnp.sum(f * f, -1, keepdims=True) for f in floats)
        scale = lax.rsqrt(square * (1.0 / (2 * half)) + EPSILON)
        for j, f in enumerate(floats):
            at = pl.multiple_of((tp if j == 0 else 1 - tp) * half, 128)
            normed[pl.ds(base, rows), pl.ds(at, half)] = (
                f * scale * gain[:, pl.ds(at, half)]
            ).astype(jnp.bfloat16)
        return 0

    lax.fori_loop(0, docs, prepare, 0)
    for b in range(blocks):
        copies[b].wait()
        at = pl.multiple_of(where[b] * depth, 128)
        left = normed[:, pl.ds(at, depth)]
        for c in range(3):
            span = pl.ds(c * cols, cols)
            part = jnp.dot(left, wbuf[b, :, span], preferred_element_type=jnp.float32)
            if b == 0:
                acc[:, span] = part
            else:
                acc[:, span] += part

    row = lax.broadcasted_iota(jnp.int32, (rows, rows), 0)
    col = lax.broadcasted_iota(jnp.int32, (rows, rows), 1)
    ordered = (col < M) | (row < M) | (col <= row)

    def one(doc, _):
        base = pl.multiple_of(doc * rows, 16)
        length = meta[turn, C_LEN + doc]
        allowed = ordered & ((col < M) | (col - M < length))
        for h in range(cols // HD):
            q, k, v = (
                acc[pl.ds(base, rows), c * cols + h * HD : c * cols + (h + 1) * HD].astype(
                    jnp.bfloat16
                )
                for c in range(3)
            )
            scores = lax.dot_general(
                q, k, (((1,), (1,)), ((), ())), preferred_element_type=jnp.float32
            ) * (1.0 / math.sqrt(HD))
            raw = jnp.where(allowed, jnp.exp(jnp.where(allowed, scores, -1e30)), 0.0)
            probs = (raw / jnp.sum(raw, -1, keepdims=True)).astype(jnp.bfloat16)
            mixed_ref[pl.ds(base, rows), h * HD : (h + 1) * HD] = jnp.dot(
                probs, v, preferred_element_type=jnp.float32
            ).astype(jnp.bfloat16)
        return 0

    lax.fori_loop(0, docs, one, 0)


def project_kernel(turn, docs, tokens, parts, pool, meta, place, mix, *refs):
    mixed = refs[:parts]
    keep, weight = refs[parts : parts + 2]
    outs = refs[parts + 2 :]
    if pool:
        out, pooled, wbuf, sems = outs
    else:
        out, wbuf, sems = outs
    rows = M + tokens
    depth = mixed[0].shape[1]
    width = keep.shape[1]
    copies = []
    for b in range(parts):
        at = pl.multiple_of(place[b] * depth, 128)
        copy = pltpu.make_async_copy(weight.at[pl.ds(at, depth), :], wbuf.at[b], sems.at[b])
        copy.start()
        copies.append(copy)
    for copy in copies:
        copy.wait()
    step = min(width, 512)
    for c in range(0, width, step):
        total = keep[:, c : c + step].astype(jnp.float32)
        for b in range(parts):
            total += jnp.dot(
                mixed[b][...], wbuf[b, :, c : c + step], preferred_element_type=jnp.float32
            )
        out[:, c : c + step] = total.astype(jnp.bfloat16)
    if pool:
        wanted = meta[turn, C_POOL] == 1
        place_row = lax.broadcasted_iota(jnp.int32, (rows, width), 0)
        for doc in range(docs):
            length = meta[turn, C_LEN + doc]
            ok = (place_row >= M) & (place_row - M < length) & wanted
            values = out[doc * rows : (doc + 1) * rows, :].astype(jnp.float32)
            summed = jnp.sum(jnp.where(ok, values, 0.0), 0, keepdims=True)
            pooled[doc : doc + 1, :] = summed * (mix[0] / jnp.maximum(length, 1).astype(jnp.float32))


def body(
    token_ids,
    seg_lengths,
    emb_table,
    mem_init,
    norm_gain,
    w_query,
    w_key,
    w_value,
    w_out,
    layer_mix,
):
    S, T, D = (lax.axis_size(a) for a in AXES)
    s, t, z = (lax.axis_index(a) for a in AXES)
    docs_local, segs, tokens = token_ids.shape
    docs = docs_local * D
    n = docs // S
    rows = M + tokens
    R = n * rows
    half = emb_table.shape[1]
    depth = w_query.shape[1]
    cols = w_query.shape[2] // 2
    lo, hi = D // 2 - 1, D // 2
    planes = (lo, hi)
    turns = segs * S + S - 1

    def lin(a, b, c):
        return (a * T + b) * D + c

    def send(block, pairs):
        return lax.ppermute(block, AXES, [(lin(*a), lin(*b)) for a, b in pairs])

    def block_of(side):
        return jnp.concatenate(
            [lax.dynamic_slice_in_dim(w[0], side * cols, cols, 1) for w in (w_query, w_key, w_value)],
            1,
        )

    weights = [block_of((z == hi).astype(jnp.int32))]
    where = [z]
    for source in range(D):
        if source == lo:
            continue
        pairs = []
        for a in range(S):
            for b in range(T):
                pairs.append(((a, b, source), (a, b, lo)))
                pairs.append(((a, b, D - 1 - source), (a, b, hi)))
        weights.append(send(block_of((z == D - 1 - source).astype(jnp.int32)), pairs))
        where.append(jnp.where(z == hi, D - 1 - source, source))
    where = jnp.stack(where).astype(jnp.int32)

    packed = jnp.concatenate([token_ids, seg_lengths[:, :, None]], 2)
    packed = lax.all_gather(packed, "doc", axis=0, tiled=True)
    ids, lengths = packed[:, :, :tokens], packed[:, :, tokens]

    vocab = emb_table.shape[0]
    tok, tok_other = [], []
    for seg in range(segs):
        local = ids[:, seg].reshape(-1) - s * vocab
        owned = (local >= 0) & (local < vocab)
        picked = jnp.take(emb_table, jnp.clip(local, 0, vocab - 1), axis=0)
        picked = jnp.where(owned[:, None], picked, jnp.zeros_like(picked))
        full = picked
        for a in range(1, S):
            full = full + send(picked, [((a, b, c), (0, b, c)) for b in range(T) for c in planes])
        tok.append(full)
        tok_other.append(send(full, [((0, b, c), (0, T - 1 - b, c)) for b in range(T) for c in planes]))
    mem_other = send(mem_init, [((0, b, c), (0, T - 1 - b, c)) for b in range(T) for c in planes])

    offset = jnp.arange(turns) - s
    group = offset % S
    segment = jnp.clip(offset // S, 0, segs - 1)
    grouped = lengths.reshape(S, n, segs)
    lens = grouped[group, :, segment]
    active = (offset >= 0) & (offset < segs * S)
    flags = jnp.stack(
        [
            jnp.full((turns,), s == 0),
            (s == 0) & (offset < S),
            jnp.full((turns,), t),
            active & (segment == segs - 1),
        ],
        1,
    ).astype(jnp.int32)
    meta = jnp.concatenate([flags, lens], 1).astype(jnp.int32)

    shifts = [(j, i) for i in range(2) for j in range(T)]
    side = (z == hi).astype(jnp.int32)
    place = jnp.stack([((t + j) % T) * 2 + (side + i) % 2 for j, i in shifts]).astype(jnp.int32)

    smem = pl.BlockSpec(memory_space=pltpu.SMEM)
    vmem = pl.BlockSpec(memory_space=pltpu.VMEM)
    anyw = pl.BlockSpec(memory_space=pl.ANY)
    out_proj = w_out[0]
    parts = len(shifts)

    own = jnp.zeros((R, half), jnp.bfloat16)
    other = jnp.zeros((R, half), jnp.bfloat16)
    pools = []
    for k in range(turns):
        g, seg = k % S, k // S
        rows_of = slice(g * n * tokens, (g + 1) * n * tokens)
        tk, tko = (a[min(seg, segs - 1)][rows_of] for a in (tok, tok_other))
        mixed, keep = pl.pallas_call(
            functools.partial(attend_kernel, k, n, tokens, D),
            out_shape=(
                jax.ShapeDtypeStruct((R, cols), jnp.bfloat16),
                jax.ShapeDtypeStruct((R, half), jnp.bfloat16),
            ),
            in_specs=[smem, smem] + [vmem] * 7 + [anyw] * D,
            out_specs=(vmem, vmem),
            scratch_shapes=[
                pltpu.VMEM((R, 2 * half), jnp.bfloat16),
                pltpu.VMEM((R, 3 * cols), jnp.float32),
                pltpu.VMEM((D, depth, 3 * cols), jnp.bfloat16),
                pltpu.SemaphoreType.DMA((D,)),
            ],
            compiler_params=pltpu.CompilerParams(vmem_limit_bytes=VMEM_LIMIT),
        )(meta, where, own, other, tk, tko, mem_init, mem_other, norm_gain, *weights)
        live = [a for a in range(S) if 0 <= k - a < segs * S]
        shared = [mixed]
        for j, i in shifts[1:]:
            pairs = [
                ((a, (b + j) % T, planes[(c + i) % 2]), (a, b, planes[c]))
                for a in live
                for b in range(T)
                for c in range(2)
            ]
            shared.append(send(mixed, pairs))
        pool = k >= (segs - 1) * S
        shapes = [jax.ShapeDtypeStruct((R, half), jnp.bfloat16)]
        if pool:
            shapes.append(jax.ShapeDtypeStruct((n, half), jnp.float32))
        result = pl.pallas_call(
            functools.partial(project_kernel, k, n, tokens, parts, pool),
            out_shape=tuple(shapes),
            in_specs=[smem, smem, smem] + [vmem] * (parts + 1) + [anyw],
            out_specs=tuple([vmem] * len(shapes)),
            scratch_shapes=[
                pltpu.VMEM((parts, cols, half), jnp.bfloat16),
                pltpu.SemaphoreType.DMA((parts,)),
            ],
            compiler_params=pltpu.CompilerParams(vmem_limit_bytes=VMEM_LIMIT),
        )(meta, place, layer_mix, *shared, keep, out_proj)
        if pool:
            pools.append(result[1])
        goes = [a for a in live if not (a == S - 1 and (k - a) // S == segs - 1)]
        if goes:
            own = send(
                result[0],
                [((a, b, c), ((a + 1) % S, b, c)) for a in goes for b in range(T) for c in planes],
            )
            other = send(
                result[0],
                [
                    ((a, b, c), ((a + 1) % S, T - 1 - b, c))
                    for a in goes
                    for b in range(T)
                    for c in planes
                ],
            )

    mine = lax.dynamic_slice_in_dim(jnp.stack(pools), s, S, 0).reshape(docs, half)
    mine = jnp.where((z == lo) | (z == hi), mine, 0.0)
    total = lax.psum(mine, "section")
    spread = total
    for k in range(1, D // 2):
        pairs = [
            ((a, b, c), (a, b, c + e)) for a in range(S) for b in range(T) for c, e in ((lo, -k), (hi, k))
        ]
        spread = spread + send(total, pairs)
    return spread


def solution(mesh):
    return jax.shard_map(
        body,
        mesh=mesh,
        in_specs=(
            P("doc", None, None),
            P("doc", None),
            P("section", "tp"),
            P(None, "tp"),
            P("section", None),
            P("section", "doc", "tp"),
            P("section", "doc", "tp"),
            P("section", "doc", "tp"),
            P("section", None, "tp"),
            P("section"),
        ),
        out_specs=P(None, "tp"),
        check_vma=False,
    )
```

```python
import functools
import math

import jax
import jax.numpy as jnp
from jax import lax
from jax.experimental import pallas as pl
from jax.experimental.pallas import tpu as pltpu
from jax.sharding import PartitionSpec as P

HD = 128
M = 16
EPSILON = 1e-05
AXES = ("section", "tp", "doc")
VMEM_LIMIT = 24 * 1024 * 1024
C_FIRST, C_INIT, C_TP, C_POOL, C_LEN = 0, 1, 2, 3, 4


def attend_kernel(
    turn, docs, tokens, blocks, meta, where, *refs
):
    halves = refs[0]
    other = refs[1]
    tok, tok_other, mem, mem_other, gain = refs[2:7]
    weights = refs[7 : 7 + blocks]
    mixed_ref, keep_ref = refs[7 + blocks : 9 + blocks]
    normed, acc = refs[9 + blocks :]
    rows = M + tokens
    half = halves.shape[1]
    depth = weights[0].shape[0]
    cols = weights[0].shape[1] // 3
    first = meta[turn, C_FIRST] == 1
    initial = meta[turn, C_INIT] == 1
    tp = meta[turn, C_TP]

    def prepare(doc, _):
        base = pl.multiple_of(doc * rows, 16)
        tbase = pl.multiple_of(doc * tokens, 16)
        parts = []
        for block, tk, mm in ((halves, tok, mem), (other, tok_other, mem_other)):
            head = jnp.where(initial, mm[...], block[pl.ds(base, M), :])
            body = jnp.where(
                first, tk[pl.ds(tbase, tokens), :], block[pl.ds(base + M, tokens), :]
            )
            parts.append(jnp.concatenate([head, body], 0))
        keep_ref[pl.ds(base, rows), :] = parts[0]
        floats = [p.astype(jnp.float32) for p in parts]
        square = sum(jnp.sum(f * f, -1, keepdims=True) for f in floats)
        scale = lax.rsqrt(square * (1.0 / (2 * half)) + EPSILON)
        for j, f in enumerate(floats):
            at = pl.multiple_of((tp if j == 0 else 1 - tp) * half, 128)
            normed[pl.ds(base, rows), pl.ds(at, half)] = (
                f * scale * gain[:, pl.ds(at, half)]
            ).astype(jnp.bfloat16)
        return 0

    lax.fori_loop(0, docs, prepare, 0)
    for b in range(blocks):
        at = pl.multiple_of(where[b] * depth, 128)
        left = normed[:, pl.ds(at, depth)]
        for c in range(3):
            span = pl.ds(c * cols, cols)
            part = jnp.dot(left, weights[b][:, span], preferred_element_type=jnp.float32)
            if b == 0:
                acc[:, span] = part
            else:
                acc[:, span] += part

    row = lax.broadcasted_iota(jnp.int32, (rows, rows), 0)
    col = lax.broadcasted_iota(jnp.int32, (rows, rows), 1)
    ordered = (col < M) | (row < M) | (col <= row)

    def one(doc, _):
        base = pl.multiple_of(doc * rows, 16)
        length = meta[turn, C_LEN + doc]
        allowed = ordered & ((col < M) | (col - M < length))
        for h in range(cols // HD):
            q, k, v = (
                acc[pl.ds(base, rows), c * cols + h * HD : c * cols + (h + 1) * HD].astype(
                    jnp.bfloat16
                )
                for c in range(3)
            )
            scores = lax.dot_general(
                q, k, (((1,), (1,)), ((), ())), preferred_element_type=jnp.float32
            ) * (1.0 / math.sqrt(HD))
            raw = jnp.where(allowed, jnp.exp(jnp.where(allowed, scores, -1e30)), 0.0)
            probs = (raw / jnp.sum(raw, -1, keepdims=True)).astype(jnp.bfloat16)
            mixed_ref[pl.ds(base, rows), h * HD : (h + 1) * HD] = jnp.dot(
                probs, v, preferred_element_type=jnp.float32
            ).astype(jnp.bfloat16)
        return 0

    lax.fori_loop(0, docs, one, 0)


def project_kernel(turn, docs, tokens, parts, pool, meta, place, mix, *refs):
    mixed = refs[:parts]
    keep, weight = refs[parts : parts + 2]
    outs = refs[parts + 2 :]
    if pool:
        out, pooled = outs
    else:
        (out,) = outs
    rows = M + tokens
    depth = mixed[0].shape[1]
    width = keep.shape[1]
    step = min(width, 512)
    for c in range(0, width, step):
        total = keep[:, c : c + step].astype(jnp.float32)
        for b in range(parts):
            at = pl.multiple_of(place[b] * depth, 128)
            total += jnp.dot(
                mixed[b][...],
                weight[pl.ds(at, depth), c : c + step],
                preferred_element_type=jnp.float32,
            )
        out[:, c : c + step] = total.astype(jnp.bfloat16)
    if pool:
        wanted = meta[turn, C_POOL] == 1
        place_row = lax.broadcasted_iota(jnp.int32, (rows, width), 0)
        for doc in range(docs):
            length = meta[turn, C_LEN + doc]
            ok = (place_row >= M) & (place_row - M < length) & wanted
            values = out[doc * rows : (doc + 1) * rows, :].astype(jnp.float32)
            summed = jnp.sum(jnp.where(ok, values, 0.0), 0, keepdims=True)
            pooled[doc : doc + 1, :] = summed * (mix[0] / jnp.maximum(length, 1).astype(jnp.float32))


def body(
    token_ids,
    seg_lengths,
    emb_table,
    mem_init,
    norm_gain,
    w_query,
    w_key,
    w_value,
    w_out,
    layer_mix,
):
    S, T, D = (lax.axis_size(a) for a in AXES)
    s, t, z = (lax.axis_index(a) for a in AXES)
    docs_local, segs, tokens = token_ids.shape
    docs = docs_local * D
    n = docs // S
    rows = M + tokens
    R = n * rows
    half = emb_table.shape[1]
    depth = w_query.shape[1]
    cols = w_query.shape[2] // 2
    lo, hi = D // 2 - 1, D // 2
    planes = (lo, hi)
    turns = segs * S + S - 1

    def lin(a, b, c):
        return (a * T + b) * D + c

    def send(block, pairs):
        return lax.ppermute(block, AXES, [(lin(*a), lin(*b)) for a, b in pairs])

    everyone = [(a, b, c) for a in range(S) for b in range(T) for c in range(D)]

    def mid(move):
        return [
            (e, move(*e) if e[2] in planes else ((e[0] + S // 2) % S, e[1], e[2])) for e in everyone
        ]

    def block_of(side):
        return jnp.concatenate(
            [lax.dynamic_slice_in_dim(w[0], side * cols, cols, 1) for w in (w_query, w_key, w_value)],
            1,
        )

    rounds = [c for c in range(D) if c != lo]
    blocks = [block_of((z == D - 1 - c).astype(jnp.int32)) for c in rounds]
    own_block = block_of((z == hi).astype(jnp.int32))
    where = jnp.stack([z] + [jnp.where(z == hi, D - 1 - c, c) for c in rounds]).astype(jnp.int32)

    def relay(parity, sent):
        moved = []
        for c, block in zip(rounds, sent):
            pairs = []
            for a in range(parity, S, 2):
                for b in range(T):
                    pairs.append(((a, b, c), (a, b, lo)))
                    pairs.append(((a, b, D - 1 - c), (a, b, hi)))
            moved.append(send(block, pairs))
        return moved

    even = relay(0, blocks)
    blocks, token_ids = lax.optimization_barrier((blocks, token_ids))
    (blocks, even) = lax.optimization_barrier((blocks, even))
    odd = relay(1, blocks)

    packed = jnp.concatenate([token_ids, seg_lengths[:, :, None]], 2)
    packed = lax.all_gather(packed, "doc", axis=0, tiled=True)
    ids, lengths = packed[:, :, :tokens], packed[:, :, tokens]

    vocab = emb_table.shape[0]
    tok, tok_other = [], []
    for seg in range(segs):
        if seg == 1:
            ids, even = lax.optimization_barrier((ids, even))
        local = ids[:, seg].reshape(-1) - s * vocab
        owned = (local >= 0) & (local < vocab)
        picked = jnp.take(emb_table, jnp.clip(local, 0, vocab - 1), axis=0)
        picked = jnp.where(owned[:, None], picked, jnp.zeros_like(picked))
        full = picked
        for a in range(1, S):
            full = full + send(picked, [((a, b, c), (0, b, c)) for b in range(T) for c in planes])
        tok.append(full)
        tok_other.append(send(full, [((0, b, c), (0, T - 1 - b, c)) for b in range(T) for c in planes]))
    mem_other = send(mem_init, [((0, b, c), (0, T - 1 - b, c)) for b in range(T) for c in planes])

    offset = jnp.arange(turns) - s
    group = offset % S
    segment = jnp.clip(offset // S, 0, segs - 1)
    grouped = lengths.reshape(S, n, segs)
    lens = grouped[group, :, segment]
    active = (offset >= 0) & (offset < segs * S)
    flags = jnp.stack(
        [
            jnp.full((turns,), s == 0),
            (s == 0) & (offset < S),
            jnp.full((turns,), t),
            active & (segment == segs - 1),
        ],
        1,
    ).astype(jnp.int32)
    meta = jnp.concatenate([flags, lens], 1).astype(jnp.int32)

    shifts = [(j, i) for i in range(2) for j in range(T)]
    side = (z == hi).astype(jnp.int32)
    place = jnp.stack([((t + j) % T) * 2 + (side + i) % 2 for j, i in shifts]).astype(jnp.int32)

    smem = pl.BlockSpec(memory_space=pltpu.SMEM)
    vmem = pl.BlockSpec(memory_space=pltpu.VMEM)
    out_proj = w_out[0]
    parts = len(shifts)

    own = jnp.zeros((R, half), jnp.bfloat16)
    other = jnp.zeros((R, half), jnp.bfloat16)
    pools = []
    weights = [own_block] + even
    for k in range(turns):
        if k == 1:
            weights = [own_block] + [a + b for a, b in zip(even, odd)]
        g, seg = k % S, k // S
        rows_of = slice(g * n * tokens, (g + 1) * n * tokens)
        tk, tko = (a[min(seg, segs - 1)][rows_of] for a in (tok, tok_other))
        mixed, keep = pl.pallas_call(
            functools.partial(attend_kernel, k, n, tokens, D),
            out_shape=(
                jax.ShapeDtypeStruct((R, cols), jnp.bfloat16),
                jax.ShapeDtypeStruct((R, half), jnp.bfloat16),
            ),
            in_specs=[smem, smem] + [vmem] * (7 + D),
            out_specs=(vmem, vmem),
            scratch_shapes=[
                pltpu.VMEM((R, 2 * half), jnp.bfloat16),
                pltpu.VMEM((R, 3 * cols), jnp.float32),
            ],
            compiler_params=pltpu.CompilerParams(vmem_limit_bytes=VMEM_LIMIT),
        )(meta, where, own, other, tk, tko, mem_init, mem_other, norm_gain, *weights)
        shared = [mixed]
        for j, i in shifts[1:]:
            def back(a, b, c):
                return (a, (b - j) % T, planes[(planes.index(c) + i) % 2])

            shared.append(send(mixed, mid(back)))
        pool = k >= (segs - 1) * S
        shapes = [jax.ShapeDtypeStruct((R, half), jnp.bfloat16)]
        if pool:
            shapes.append(jax.ShapeDtypeStruct((n, half), jnp.float32))
        result = pl.pallas_call(
            functools.partial(project_kernel, k, n, tokens, parts, pool),
            out_shape=tuple(shapes),
            in_specs=[smem, smem, smem] + [vmem] * (parts + 2),
            out_specs=tuple([vmem] * len(shapes)),
            compiler_params=pltpu.CompilerParams(vmem_limit_bytes=VMEM_LIMIT),
        )(meta, place, layer_mix, *shared, keep, out_proj)
        if pool:
            pools.append(result[1])
        if k < turns - 1:
            own = send(result[0], [(e, ((e[0] + 1) % S, e[1], e[2])) for e in everyone])
            other = send(result[0], [(e, ((e[0] + 1) % S, T - 1 - e[1], e[2])) for e in everyone])

    mine = lax.dynamic_slice_in_dim(jnp.stack(pools), s, S, 0).reshape(docs, half)
    total = mine
    for a in range(1, S):
        total = total + send(mine, [(e, ((e[0] + a) % S, e[1], e[2])) for e in everyone])
    spread = total
    for k in range(1, D // 2):
        ends = ((lo, lo - k), (hi, hi + k))
        pairs = [((a, b, c), (a, b, e)) for a in range(S) for b in range(T) for c, e in ends]
        got = send(total, pairs + [(e, c) for c, e in pairs])
        spread = jnp.where((z == lo - k) | (z == hi + k), got, spread)
    return spread


def solution(mesh):
    return jax.shard_map(
        body,
        mesh=mesh,
        in_specs=(
            P("doc", None, None),
            P("doc", None),
            P("section", "tp"),
            P(None, "tp"),
            P("section", None),
            P("section", "doc", "tp"),
            P("section", "doc", "tp"),
            P("section", "doc", "tp"),
            P("section", None, "tp"),
            P("section"),
        ),
        out_specs=P(None, "tp"),
        check_vma=False,
    )
```

```python
import functools
import math

import jax
import jax.numpy as jnp
from jax import lax
from jax.experimental import pallas as pl
from jax.experimental.pallas import tpu as pltpu
from jax.sharding import PartitionSpec as P

HD = 128
M = 16
EPSILON = 1e-05
AXES = ("section", "tp", "doc")
C_FIRST, C_INIT, C_TP, C_POOL, C_PHASE, C_LEN = 0, 1, 2, 3, 4, 5


def attend_kernel(turn, docs, tokens, blocks, sets, meta, where, *refs):
    halves = refs[0]
    other = refs[1]
    tok, tok_other, mem, mem_other, gain = refs[2:7]
    held = 1 + sets * (blocks - 1)
    weights = refs[7 : 7 + held]
    mixed_ref, keep_ref = refs[7 + held : 9 + held]
    normed, acc = refs[9 + held :]
    rows = M + tokens
    half = halves.shape[1]
    depth = weights[0].shape[0]
    cols = weights[0].shape[1] // 3
    first = meta[turn, C_FIRST] == 1
    initial = meta[turn, C_INIT] == 1
    tp = meta[turn, C_TP]

    def prepare(doc, _):
        base = pl.multiple_of(doc * rows, 16)
        tbase = pl.multiple_of(doc * tokens, 16)
        parts = []
        for block, tk, mm in ((halves, tok, mem), (other, tok_other, mem_other)):
            head = jnp.where(initial, mm[...], block[pl.ds(base, M), :])
            body = jnp.where(
                first, tk[pl.ds(tbase, tokens), :], block[pl.ds(base + M, tokens), :]
            )
            parts.append(jnp.concatenate([head, body], 0))
        keep_ref[pl.ds(base, rows), :] = parts[0]
        floats = [p.astype(jnp.float32) for p in parts]
        square = sum(jnp.sum(f * f, -1, keepdims=True) for f in floats)
        scale = lax.rsqrt(square * (1.0 / (2 * half)) + EPSILON)
        for j, f in enumerate(floats):
            at = pl.multiple_of((tp if j == 0 else 1 - tp) * half, 128)
            normed[pl.ds(base, rows), pl.ds(at, half)] = (
                f * scale * gain[:, pl.ds(at, half)]
            ).astype(jnp.bfloat16)
        return 0

    lax.fori_loop(0, docs, prepare, 0)

    def multiply(b, weight):
        at = pl.multiple_of(where[b] * depth, 128)
        left = normed[:, pl.ds(at, depth)]
        for c in range(3):
            span = pl.ds(c * cols, cols)
            part = jnp.dot(left, weight[:, span], preferred_element_type=jnp.float32)
            if b == 0:
                acc[:, span] = part
            else:
                acc[:, span] += part

    multiply(0, weights[0])
    for phase in range(sets):

        def received(phase=phase):
            for b in range(1, blocks):
                multiply(b, weights[b + phase * (blocks - 1)])

        if sets == 1:
            received()
        else:
            pl.when(meta[turn, C_PHASE] == phase)(received)

    row = lax.broadcasted_iota(jnp.int32, (rows, rows), 0)
    col = lax.broadcasted_iota(jnp.int32, (rows, rows), 1)
    ordered = (col < M) | (row < M) | (col <= row)

    def one(doc, _):
        base = pl.multiple_of(doc * rows, 16)
        length = meta[turn, C_LEN + doc]
        allowed = ordered & ((col < M) | (col - M < length))
        for h in range(cols // HD):
            q, k, v = (
                acc[pl.ds(base, rows), c * cols + h * HD : c * cols + (h + 1) * HD].astype(
                    jnp.bfloat16
                )
                for c in range(3)
            )
            scores = lax.dot_general(
                q, k, (((1,), (1,)), ((), ())), preferred_element_type=jnp.float32
            ) * (1.0 / math.sqrt(HD))
            raw = jnp.where(allowed, jnp.exp(jnp.where(allowed, scores, -1e30)), 0.0)
            probs = (raw / jnp.sum(raw, -1, keepdims=True)).astype(jnp.bfloat16)
            mixed_ref[pl.ds(base, rows), h * HD : (h + 1) * HD] = jnp.dot(
                probs, v, preferred_element_type=jnp.float32
            ).astype(jnp.bfloat16)
        return 0

    lax.fori_loop(0, docs, one, 0)


def project_kernel(turn, docs, tokens, parts, pool, meta, place, mix, *refs):
    mixed = refs[:parts]
    keep, weight = refs[parts : parts + 2]
    outs = refs[parts + 2 :]
    if pool:
        out, pooled = outs
    else:
        (out,) = outs
    rows = M + tokens
    depth = mixed[0].shape[1]
    width = keep.shape[1]
    step = min(width, 512)
    for c in range(0, width, step):
        total = keep[:, c : c + step].astype(jnp.float32)
        for b in range(parts):
            at = pl.multiple_of(place[b] * depth, 128)
            total += jnp.dot(
                mixed[b][...],
                weight[pl.ds(at, depth), c : c + step],
                preferred_element_type=jnp.float32,
            )
        out[:, c : c + step] = total.astype(jnp.bfloat16)
    if pool:
        wanted = meta[turn, C_POOL] == 1
        place_row = lax.broadcasted_iota(jnp.int32, (rows, width), 0)
        for doc in range(docs):
            length = meta[turn, C_LEN + doc]
            ok = (place_row >= M) & (place_row - M < length) & wanted
            values = out[doc * rows : (doc + 1) * rows, :].astype(jnp.float32)
            summed = jnp.sum(jnp.where(ok, values, 0.0), 0, keepdims=True)
            pooled[doc : doc + 1, :] = summed * (mix[0] / jnp.maximum(length, 1).astype(jnp.float32))


def body(
    token_ids,
    seg_lengths,
    emb_table,
    mem_init,
    norm_gain,
    w_query,
    w_key,
    w_value,
    w_out,
    layer_mix,
):
    S, T, D = (lax.axis_size(a) for a in AXES)
    s, t, z = (lax.axis_index(a) for a in AXES)
    docs_local, segs, tokens = token_ids.shape
    docs = docs_local * D
    n = docs // S
    rows = M + tokens
    R = n * rows
    half = emb_table.shape[1]
    depth = w_query.shape[1]
    cols = w_query.shape[2] // 2
    lo, hi = D // 2 - 1, D // 2
    planes = (lo, hi)
    turns = segs * S + S - 1

    def lin(a, b, c):
        return (a * T + b) * D + c

    limit = 24 * 2**20 + 2 * R * (4 * half + 12 * cols)
    params = pltpu.CompilerParams(vmem_limit_bytes=limit)

    def send(block, pairs):
        return lax.ppermute(block, AXES, [(lin(*a), lin(*b)) for a, b in pairs])

    everyone = [(a, b, c) for a in range(S) for b in range(T) for c in range(D)]

    def mid(move):
        return [
            (e, move(*e) if e[2] in planes else ((e[0] + S // 2) % S, e[1], e[2])) for e in everyone
        ]

    packed = jnp.concatenate([token_ids, seg_lengths[:, :, None]], 2)
    gathered = [packed]
    for k in range(1, D):
        gathered.append(send(packed, [(e, (e[0], e[1], (e[2] + k) % D)) for e in everyone]))
    source = (z - jnp.arange(D)) % D
    chosen = (source[None, :] == jnp.arange(D)[:, None])[:, :, None, None, None]
    gathered = jnp.sum(jnp.where(chosen, jnp.stack(gathered)[None], 0), 1)
    packed = gathered.reshape(docs, segs, tokens + 1)
    ids, lengths = packed[:, :, :tokens], packed[:, :, tokens]

    def block_of(side):
        return jnp.concatenate(
            [lax.dynamic_slice_in_dim(w[0], side * cols, cols, 1) for w in (w_query, w_key, w_value)],
            1,
        )

    rounds = [c for c in range(D) if c != lo]
    blocks = [block_of((z == D - 1 - c).astype(jnp.int32)) for c in rounds]
    own_block = block_of((z == hi).astype(jnp.int32))
    where = jnp.stack([z] + [jnp.where(z == hi, D - 1 - c, c) for c in rounds]).astype(jnp.int32)

    def relay(parity, sent):
        moved = []
        for c, block in zip(rounds, sent):
            pairs = []
            for a in range(parity, S, 2):
                for b in range(T):
                    pairs.append(((a, b, c), (a, b, lo)))
                    pairs.append(((a, b, D - 1 - c), (a, b, hi)))
            moved.append(send(block, pairs))
        return moved

    vocab = emb_table.shape[0]

    def embed(index):
        local = index.reshape(-1) - s * vocab
        owned = (local >= 0) & (local < vocab)
        picked = jnp.take(emb_table, jnp.clip(local, 0, vocab - 1), axis=0)
        picked = jnp.where(owned[:, None], picked, jnp.zeros_like(picked))
        full = picked
        for a in range(1, S):
            full = full + send(picked, [((a, b, c), (0, b, c)) for b in range(T) for c in planes])
        return full, send(full, [((0, b, c), (0, T - 1 - b, c)) for b in range(T) for c in planes])

    ids, blocks = lax.optimization_barrier((ids, blocks))
    even = relay(0, blocks)
    pairs = [embed(ids[:, 0])]
    mem_other = send(mem_init, [((0, b, c), (0, T - 1 - b, c)) for b in range(T) for c in planes])
    blocks, even, pairs, mem_other, ids = lax.optimization_barrier(
        (blocks, even, pairs, mem_other, ids)
    )
    odd = relay(1, blocks)
    for seg in range(1, segs):
        pairs.append(embed(ids[:, seg]))
    tok, tok_other = zip(*pairs)

    offset = jnp.arange(turns) - s
    group = offset % S
    segment = jnp.clip(offset // S, 0, segs - 1)
    grouped = lengths.reshape(S, n, segs)
    lens = grouped[group, :, segment]
    active = (offset >= 0) & (offset < segs * S)
    flags = jnp.stack(
        [
            jnp.full((turns,), s == 0),
            (s == 0) & (offset < S),
            jnp.full((turns,), t),
            active & (segment == segs - 1),
            jnp.full((turns,), s % 2),
        ],
        1,
    ).astype(jnp.int32)
    meta = jnp.concatenate([flags, lens], 1).astype(jnp.int32)

    shifts = [(j, i) for i in range(2) for j in range(T)]
    side = (z == hi).astype(jnp.int32)
    place = jnp.stack([((t + j) % T) * 2 + (side + i) % 2 for j, i in shifts]).astype(jnp.int32)

    smem = pl.BlockSpec(memory_space=pltpu.SMEM)
    vmem = pl.BlockSpec(memory_space=pltpu.VMEM)
    out_proj = w_out[0]
    parts = len(shifts)

    own = jnp.zeros((R, half), jnp.bfloat16)
    other = jnp.zeros((R, half), jnp.bfloat16)
    pools = []
    for k in range(turns):
        sets = 1 if k == 0 else 2
        weights = [own_block] + even + (odd if k else [])
        g, seg = k % S, k // S
        rows_of = slice(g * n * tokens, (g + 1) * n * tokens)
        tk, tko = (a[min(seg, segs - 1)][rows_of] for a in (tok, tok_other))
        mixed, keep = pl.pallas_call(
            functools.partial(attend_kernel, k, n, tokens, D, sets),
            out_shape=(
                jax.ShapeDtypeStruct((R, cols), jnp.bfloat16),
                jax.ShapeDtypeStruct((R, half), jnp.bfloat16),
            ),
            in_specs=[smem, smem] + [vmem] * (7 + len(weights)),
            out_specs=(vmem, vmem),
            scratch_shapes=[
                pltpu.VMEM((R, 2 * half), jnp.bfloat16),
                pltpu.VMEM((R, 3 * cols), jnp.float32),
            ],
            compiler_params=params,
        )(meta, where, own, other, tk, tko, mem_init, mem_other, norm_gain, *weights)
        shared = [mixed]
        for j, i in shifts[1:]:
            def back(a, b, c):
                return (a, (b - j) % T, planes[(planes.index(c) + i) % 2])

            shared.append(send(mixed, mid(back)))
        pool = k >= (segs - 1) * S
        shapes = [jax.ShapeDtypeStruct((R, half), jnp.bfloat16)]
        if pool:
            shapes.append(jax.ShapeDtypeStruct((n, half), jnp.float32))
        result = pl.pallas_call(
            functools.partial(project_kernel, k, n, tokens, parts, pool),
            out_shape=tuple(shapes),
            in_specs=[smem, smem, smem] + [vmem] * (parts + 2),
            out_specs=tuple([vmem] * len(shapes)),
            compiler_params=params,
        )(meta, place, layer_mix, *shared, keep, out_proj)
        if pool:
            pools.append(result[1])
        if k < turns - 1:
            own = send(result[0], [(e, ((e[0] + 1) % S, e[1], e[2])) for e in everyone])
            other = send(result[0], [(e, ((e[0] + 1) % S, T - 1 - e[1], e[2])) for e in everyone])

    mine = lax.dynamic_slice_in_dim(jnp.stack(pools), s, S, 0).reshape(docs, half)
    total = mine
    for a in range(1, S):
        total = total + send(mine, [(e, ((e[0] + a) % S, e[1], e[2])) for e in everyone])
    spread = total
    for k in range(1, D // 2):
        ends = ((lo, lo - k), (hi, hi + k))
        pairs = [((a, b, c), (a, b, e)) for a in range(S) for b in range(T) for c, e in ends]
        got = send(total, pairs + [(e, c) for c, e in pairs])
        spread = jnp.where((z == lo - k) | (z == hi + k), got, spread)
    return spread


def solution(mesh):
    return jax.shard_map(
        body,
        mesh=mesh,
        in_specs=(
            P("doc", None, None),
            P("doc", None),
            P("section", "tp"),
            P(None, "tp"),
            P("section", None),
            P("section", "doc", "tp"),
            P("section", "doc", "tp"),
            P("section", "doc", "tp"),
            P("section", None, "tp"),
            P("section"),
        ),
        out_specs=P(None, "tp"),
        check_vma=False,
    )
```

```python
import functools
import math

import jax
import jax.numpy as jnp
from jax import lax
from jax.experimental import pallas as pl
from jax.experimental.pallas import tpu as pltpu
from jax.sharding import PartitionSpec as P

HD = 128
M = 16
EPSILON = 1e-05
AXES = ("section", "tp", "doc")
C_FIRST, C_INIT, C_TP, C_POOL, C_LEN = 0, 1, 2, 3, 4


def attend_kernel(turn, docs, tokens, blocks, meta, where, *refs):
    halves = refs[0]
    other = refs[1]
    tok, tok_other, mem, mem_other, gain = refs[2:7]
    weights = refs[7 : 7 + blocks]
    mixed_ref, keep_ref = refs[7 + blocks : 9 + blocks]
    normed, acc = refs[9 + blocks :]
    rows = M + tokens
    half = halves.shape[1]
    depth = weights[0].shape[0]
    cols = weights[0].shape[1] // 3
    first = meta[turn, C_FIRST] == 1
    initial = meta[turn, C_INIT] == 1
    tp = meta[turn, C_TP]

    def prepare(doc, _):
        base = pl.multiple_of(doc * rows, 16)
        tbase = pl.multiple_of(doc * tokens, 16)
        parts = []
        for block, tk, mm in ((halves, tok, mem), (other, tok_other, mem_other)):
            head = jnp.where(initial, mm[...], block[pl.ds(base, M), :])
            body = jnp.where(
                first, tk[pl.ds(tbase, tokens), :], block[pl.ds(base + M, tokens), :]
            )
            parts.append(jnp.concatenate([head, body], 0))
        keep_ref[pl.ds(base, rows), :] = parts[0]
        floats = [p.astype(jnp.float32) for p in parts]
        square = sum(jnp.sum(f * f, -1, keepdims=True) for f in floats)
        scale = lax.rsqrt(square * (1.0 / (2 * half)) + EPSILON)
        for j, f in enumerate(floats):
            at = pl.multiple_of((tp if j == 0 else 1 - tp) * half, 128)
            normed[pl.ds(base, rows), pl.ds(at, half)] = (
                f * scale * gain[:, pl.ds(at, half)]
            ).astype(jnp.bfloat16)
        return 0

    lax.fori_loop(0, docs, prepare, 0)
    for b in range(blocks):
        at = pl.multiple_of(where[b] * depth, 128)
        left = normed[:, pl.ds(at, depth)]
        for c in range(3):
            span = pl.ds(c * cols, cols)
            part = jnp.dot(left, weights[b][:, span], preferred_element_type=jnp.float32)
            if b == 0:
                acc[:, span] = part
            else:
                acc[:, span] += part

    row = lax.broadcasted_iota(jnp.int32, (rows, rows), 0)
    col = lax.broadcasted_iota(jnp.int32, (rows, rows), 1)
    ordered = (col < M) | (row < M) | (col <= row)

    def one(doc, _):
        base = pl.multiple_of(doc * rows, 16)
        length = meta[turn, C_LEN + doc]
        allowed = ordered & ((col < M) | (col - M < length))
        for h in range(cols // HD):
            q, k, v = (
                acc[pl.ds(base, rows), c * cols + h * HD : c * cols + (h + 1) * HD].astype(
                    jnp.bfloat16
                )
                for c in range(3)
            )
            scores = lax.dot_general(
                q, k, (((1,), (1,)), ((), ())), preferred_element_type=jnp.float32
            ) * (1.0 / math.sqrt(HD))
            raw = jnp.where(allowed, jnp.exp(jnp.where(allowed, scores, -1e30)), 0.0)
            probs = (raw / jnp.sum(raw, -1, keepdims=True)).astype(jnp.bfloat16)
            mixed_ref[pl.ds(base, rows), h * HD : (h + 1) * HD] = jnp.dot(
                probs, v, preferred_element_type=jnp.float32
            ).astype(jnp.bfloat16)
        return 0

    lax.fori_loop(0, docs, one, 0)


def choose_kernel(count, phase, *refs):
    outs, sems = refs[2 * count : 3 * count], refs[3 * count]
    for p in range(2):

        @pl.when(phase[0] == p)
        def _(p=p):
            copies = [
                pltpu.make_async_copy(refs[p * count + b], outs[b], sems.at[b])
                for b in range(count)
            ]
            for copy in copies:
                copy.start()
            for copy in copies:
                copy.wait()


def project_kernel(turn, docs, tokens, parts, pool, meta, place, mix, *refs):
    mixed = refs[:parts]
    keep, weight = refs[parts : parts + 2]
    outs = refs[parts + 2 :]
    if pool:
        out, pooled = outs
    else:
        (out,) = outs
    rows = M + tokens
    depth = mixed[0].shape[1]
    width = keep.shape[1]
    step = min(width, 512)
    for c in range(0, width, step):
        total = keep[:, c : c + step].astype(jnp.float32)
        for b in range(parts):
            at = pl.multiple_of(place[b] * depth, 128)
            total += jnp.dot(
                mixed[b][...],
                weight[pl.ds(at, depth), c : c + step],
                preferred_element_type=jnp.float32,
            )
        out[:, c : c + step] = total.astype(jnp.bfloat16)
    if pool:
        wanted = meta[turn, C_POOL] == 1
        place_row = lax.broadcasted_iota(jnp.int32, (rows, width), 0)
        for doc in range(docs):
            length = meta[turn, C_LEN + doc]
            ok = (place_row >= M) & (place_row - M < length) & wanted
            values = out[doc * rows : (doc + 1) * rows, :].astype(jnp.float32)
            summed = jnp.sum(jnp.where(ok, values, 0.0), 0, keepdims=True)
            pooled[doc : doc + 1, :] = summed * (mix[0] / jnp.maximum(length, 1).astype(jnp.float32))


def body(
    token_ids,
    seg_lengths,
    emb_table,
    mem_init,
    norm_gain,
    w_query,
    w_key,
    w_value,
    w_out,
    layer_mix,
):
    S, T, D = (lax.axis_size(a) for a in AXES)
    s, t, z = (lax.axis_index(a) for a in AXES)
    docs_local, segs, tokens = token_ids.shape
    docs = docs_local * D
    n = docs // S
    rows = M + tokens
    R = n * rows
    half = emb_table.shape[1]
    depth = w_query.shape[1]
    cols = w_query.shape[2] // 2
    lo, hi = D // 2 - 1, D // 2
    planes = (lo, hi)
    turns = segs * S + S - 1

    def lin(a, b, c):
        return (a * T + b) * D + c

    limit = 20 * 2**20 + 2 * R * (4 * half + 12 * cols)
    params = pltpu.CompilerParams(vmem_limit_bytes=limit)

    def send(block, pairs):
        return lax.ppermute(block, AXES, [(lin(*a), lin(*b)) for a, b in pairs])

    everyone = [(a, b, c) for a in range(S) for b in range(T) for c in range(D)]

    def mid(move):
        return [
            (e, move(*e) if e[2] in planes else ((e[0] + S // 2) % S, e[1], e[2])) for e in everyone
        ]

    packed = jnp.concatenate([token_ids, seg_lengths[:, :, None]], 2)
    gathered = [packed]
    for k in range(1, D):
        gathered.append(send(packed, [(e, (e[0], e[1], (e[2] + k) % D)) for e in everyone]))
    source = (z - jnp.arange(D)) % D
    chosen = (source[None, :] == jnp.arange(D)[:, None])[:, :, None, None, None]
    gathered = jnp.sum(jnp.where(chosen, jnp.stack(gathered)[None], 0), 1)
    packed = gathered.reshape(docs, segs, tokens + 1)
    ids, lengths = packed[:, :, :tokens], packed[:, :, tokens]

    def block_of(side):
        return jnp.concatenate(
            [lax.dynamic_slice_in_dim(w[0], side * cols, cols, 1) for w in (w_query, w_key, w_value)],
            1,
        )

    rounds = [c for c in range(D) if c != lo]
    blocks = [block_of((z == D - 1 - c).astype(jnp.int32)) for c in rounds]
    own_block = block_of((z == hi).astype(jnp.int32))
    where = jnp.stack([z] + [jnp.where(z == hi, D - 1 - c, c) for c in rounds]).astype(jnp.int32)

    def relay(parity, sent):
        moved = []
        for c, block in zip(rounds, sent):
            pairs = []
            for a in range(parity, S, 2):
                for b in range(T):
                    pairs.append(((a, b, c), (a, b, lo)))
                    pairs.append(((a, b, D - 1 - c), (a, b, hi)))
            moved.append(send(block, pairs))
        return moved

    vocab = emb_table.shape[0]

    def embed(index):
        local = index.reshape(-1) - s * vocab
        owned = (local >= 0) & (local < vocab)
        picked = jnp.take(emb_table, jnp.clip(local, 0, vocab - 1), axis=0)
        picked = jnp.where(owned[:, None], picked, jnp.zeros_like(picked))
        full = picked
        for a in range(1, S):
            full = full + send(picked, [((a, b, c), (0, b, c)) for b in range(T) for c in planes])
        return full, send(full, [((0, b, c), (0, T - 1 - b, c)) for b in range(T) for c in planes])

    first_ids = ids[:n, 0]
    rest_ids = jnp.concatenate([ids[n:, 0]] + [ids[:, seg] for seg in range(1, segs)])
    even = relay(0, blocks)
    tok_first = embed(first_ids)
    mem_other = send(mem_init, [((0, b, c), (0, T - 1 - b, c)) for b in range(T) for c in planes])
    gate = sum(e[:M, :HD].astype(jnp.float32) for e in even).astype(jnp.bfloat16)
    gate = send(gate, [(e, (e[0] ^ 1, e[1], e[2])) for e in everyone])
    blocks, gate, even, tok_first, mem_other, rest_ids = lax.optimization_barrier(
        (blocks, gate, even, tok_first, mem_other, rest_ids)
    )
    odd = relay(1, blocks)
    zero = jnp.minimum(jnp.abs(gate[0, 0]), 0).astype(jnp.int32)
    tok_rest = embed(rest_ids + zero)

    offset = jnp.arange(turns) - s
    group = offset % S
    segment = jnp.clip(offset // S, 0, segs - 1)
    grouped = lengths.reshape(S, n, segs)
    lens = grouped[group, :, segment]
    active = (offset >= 0) & (offset < segs * S)
    flags = jnp.stack(
        [
            jnp.full((turns,), s == 0),
            (s == 0) & (offset < S),
            jnp.full((turns,), t),
            active & (segment == segs - 1),
        ],
        1,
    ).astype(jnp.int32)
    meta = jnp.concatenate([flags, lens], 1).astype(jnp.int32)

    shifts = [(j, i) for i in range(2) for j in range(T)]
    side = (z == hi).astype(jnp.int32)
    place = jnp.stack([((t + j) % T) * 2 + (side + i) % 2 for j, i in shifts]).astype(jnp.int32)

    smem = pl.BlockSpec(memory_space=pltpu.SMEM)
    vmem = pl.BlockSpec(memory_space=pltpu.VMEM)
    out_proj = w_out[0]
    parts = len(shifts)

    own = jnp.zeros((R, half), jnp.bfloat16)
    other = jnp.zeros((R, half), jnp.bfloat16)
    pools = []
    for k in range(turns):
        if k == 0:
            weights = [own_block] + even
            tk, tko = tok_first
        elif k == 1:
            count = len(even)
            weights = [own_block] + list(
                pl.pallas_call(
                    functools.partial(choose_kernel, count),
                    out_shape=[jax.ShapeDtypeStruct(e.shape, e.dtype) for e in even],
                    in_specs=[smem] + [pl.BlockSpec(memory_space=pl.ANY)] * (2 * count),
                    out_specs=[vmem] * count,
                    scratch_shapes=[pltpu.SemaphoreType.DMA((count,))],
                    compiler_params=params,
                )((s % 2).astype(jnp.int32).reshape(1), *even, *odd)
            )
        if k > 0:
            step = n * tokens
            at = min(k, segs * S - 1) - 1
            tk, tko = (a[at * step : (at + 1) * step] for a in tok_rest)
        mixed, keep = pl.pallas_call(
            functools.partial(attend_kernel, k, n, tokens, D),
            out_shape=(
                jax.ShapeDtypeStruct((R, cols), jnp.bfloat16),
                jax.ShapeDtypeStruct((R, half), jnp.bfloat16),
            ),
            in_specs=[smem, smem] + [vmem] * (7 + len(weights)),
            out_specs=(vmem, vmem),
            scratch_shapes=[
                pltpu.VMEM((R, 2 * half), jnp.bfloat16),
                pltpu.VMEM((R, 3 * cols), jnp.float32),
            ],
            compiler_params=params,
        )(meta, where, own, other, tk, tko, mem_init, mem_other, norm_gain, *weights)
        shared = [mixed]
        for j, i in shifts[1:]:
            def back(a, b, c):
                return (a, (b - j) % T, planes[(planes.index(c) + i) % 2])

            shared.append(send(mixed, mid(back)))
        pool = k >= (segs - 1) * S
        shapes = [jax.ShapeDtypeStruct((R, half), jnp.bfloat16)]
        if pool:
            shapes.append(jax.ShapeDtypeStruct((n, half), jnp.float32))
        result = pl.pallas_call(
            functools.partial(project_kernel, k, n, tokens, parts, pool),
            out_shape=tuple(shapes),
            in_specs=[smem, smem, smem] + [vmem] * (parts + 2),
            out_specs=tuple([vmem] * len(shapes)),
            compiler_params=params,
        )(meta, place, layer_mix, *shared, keep, out_proj)
        if pool:
            pools.append(result[1])
        if k < turns - 1:
            own = send(result[0], [(e, ((e[0] + 1) % S, e[1], e[2])) for e in everyone])
            other = send(result[0], [(e, ((e[0] + 1) % S, T - 1 - e[1], e[2])) for e in everyone])

    mine = lax.dynamic_slice_in_dim(jnp.stack(pools), s, S, 0).reshape(docs, half)
    total = mine
    for a in range(1, S):
        total = total + send(mine, [(e, ((e[0] + a) % S, e[1], e[2])) for e in everyone])
    spread = total
    for k in range(1, D // 2):
        ends = ((lo, lo - k), (hi, hi + k))
        pairs = [((a, b, c), (a, b, e)) for a in range(S) for b in range(T) for c, e in ends]
        got = send(total, pairs + [(e, c) for c, e in pairs])
        spread = jnp.where((z == lo - k) | (z == hi + k), got, spread)
    return spread


def solution(mesh):
    return jax.shard_map(
        body,
        mesh=mesh,
        in_specs=(
            P("doc", None, None),
            P("doc", None),
            P("section", "tp"),
            P(None, "tp"),
            P("section", None),
            P("section", "doc", "tp"),
            P("section", "doc", "tp"),
            P("section", "doc", "tp"),
            P("section", None, "tp"),
            P("section"),
        ),
        out_specs=P(None, "tp"),
        check_vma=False,
    )
```

```python
import functools
import math

import jax
import jax.numpy as jnp
from jax import lax
from jax.experimental import pallas as pl
from jax.experimental.pallas import tpu as pltpu
from jax.sharding import PartitionSpec as P

HD = 128
M = 16
EPSILON = 1e-05
AXES = ("section", "tp", "doc")
C_FIRST, C_INIT, C_TP, C_POOL, C_LEN = 0, 1, 2, 3, 4


def attend_kernel(turn, docs, tokens, blocks, meta, where, *refs):
    halves = refs[0]
    other = refs[1]
    tok, tok_other, mem, mem_other, gain = refs[2:7]
    weights = refs[7 : 7 + blocks]
    mixed_ref, keep_ref = refs[7 + blocks : 9 + blocks]
    normed, acc = refs[9 + blocks :]
    rows = M + tokens
    half = halves.shape[1]
    depth = weights[0].shape[0]
    cols = weights[0].shape[1] // 3
    first = meta[turn, C_FIRST] == 1
    initial = meta[turn, C_INIT] == 1
    tp = meta[turn, C_TP]

    def prepare(doc, _):
        base = pl.multiple_of(doc * rows, 16)
        tbase = pl.multiple_of(doc * tokens, 16)
        parts = []
        for block, tk, mm in ((halves, tok, mem), (other, tok_other, mem_other)):
            head = jnp.where(initial, mm[...], block[pl.ds(base, M), :])
            body = jnp.where(
                first, tk[pl.ds(tbase, tokens), :], block[pl.ds(base + M, tokens), :]
            )
            parts.append(jnp.concatenate([head, body], 0))
        keep_ref[pl.ds(base, rows), :] = parts[0]
        floats = [p.astype(jnp.float32) for p in parts]
        square = sum(jnp.sum(f * f, -1, keepdims=True) for f in floats)
        scale = lax.rsqrt(square * (1.0 / (2 * half)) + EPSILON)
        for j, f in enumerate(floats):
            at = pl.multiple_of((tp if j == 0 else 1 - tp) * half, 128)
            normed[pl.ds(base, rows), pl.ds(at, half)] = (
                f * scale * gain[:, pl.ds(at, half)]
            ).astype(jnp.bfloat16)
        return 0

    lax.fori_loop(0, docs, prepare, 0)
    for b in range(blocks):
        at = pl.multiple_of(where[b] * depth, 128)
        left = normed[:, pl.ds(at, depth)]
        for c in range(3):
            span = pl.ds(c * cols, cols)
            part = jnp.dot(left, weights[b][:, span], preferred_element_type=jnp.float32)
            if b == 0:
                acc[:, span] = part
            else:
                acc[:, span] += part

    row = lax.broadcasted_iota(jnp.int32, (rows, rows), 0)
    col = lax.broadcasted_iota(jnp.int32, (rows, rows), 1)
    ordered = (col < M) | (row < M) | (col <= row)

    def one(doc, _):
        base = pl.multiple_of(doc * rows, 16)
        length = meta[turn, C_LEN + doc]
        allowed = ordered & ((col < M) | (col - M < length))
        for h in range(cols // HD):
            q, k, v = (
                acc[pl.ds(base, rows), c * cols + h * HD : c * cols + (h + 1) * HD].astype(
                    jnp.bfloat16
                )
                for c in range(3)
            )
            scores = lax.dot_general(
                q, k, (((1,), (1,)), ((), ())), preferred_element_type=jnp.float32
            ) * (1.0 / math.sqrt(HD))
            raw = jnp.where(allowed, jnp.exp(jnp.where(allowed, scores, -1e30)), 0.0)
            probs = (raw / jnp.sum(raw, -1, keepdims=True)).astype(jnp.bfloat16)
            mixed_ref[pl.ds(base, rows), h * HD : (h + 1) * HD] = jnp.dot(
                probs, v, preferred_element_type=jnp.float32
            ).astype(jnp.bfloat16)
        return 0

    lax.fori_loop(0, docs, one, 0)


def choose_kernel(count, phase, *refs):
    outs, sems = refs[2 * count : 3 * count], refs[3 * count]
    for p in range(2):

        @pl.when(phase[0] == p)
        def _(p=p):
            copies = [
                pltpu.make_async_copy(refs[p * count + b], outs[b], sems.at[b])
                for b in range(count)
            ]
            for copy in copies:
                copy.start()
            for copy in copies:
                copy.wait()


def project_kernel(turn, docs, tokens, parts, pool, meta, place, mix, *refs):
    mixed = refs[:parts]
    keep, weight = refs[parts : parts + 2]
    outs = refs[parts + 2 :]
    if pool:
        out, pooled = outs
    else:
        (out,) = outs
    rows = M + tokens
    depth = mixed[0].shape[1]
    width = keep.shape[1]
    step = min(width, 512)
    for c in range(0, width, step):
        total = keep[:, c : c + step].astype(jnp.float32)
        for b in range(parts):
            at = pl.multiple_of(place[b] * depth, 128)
            total += jnp.dot(
                mixed[b][...],
                weight[pl.ds(at, depth), c : c + step],
                preferred_element_type=jnp.float32,
            )
        out[:, c : c + step] = total.astype(jnp.bfloat16)
    if pool:
        wanted = meta[turn, C_POOL] == 1
        place_row = lax.broadcasted_iota(jnp.int32, (rows, width), 0)
        for doc in range(docs):
            length = meta[turn, C_LEN + doc]
            ok = (place_row >= M) & (place_row - M < length) & wanted
            values = out[doc * rows : (doc + 1) * rows, :].astype(jnp.float32)
            summed = jnp.sum(jnp.where(ok, values, 0.0), 0, keepdims=True)
            pooled[doc : doc + 1, :] = summed * (mix[0] / jnp.maximum(length, 1).astype(jnp.float32))


def body(
    token_ids,
    seg_lengths,
    emb_table,
    mem_init,
    norm_gain,
    w_query,
    w_key,
    w_value,
    w_out,
    layer_mix,
):
    S, T, D = (lax.axis_size(a) for a in AXES)
    s, t, z = (lax.axis_index(a) for a in AXES)
    docs_local, segs, tokens = token_ids.shape
    docs = docs_local * D
    n = docs // S
    rows = M + tokens
    R = n * rows
    half = emb_table.shape[1]
    depth = w_query.shape[1]
    cols = w_query.shape[2] // 2
    lo, hi = D // 2 - 1, D // 2
    planes = (lo, hi)
    turns = segs * S + S - 1

    def lin(a, b, c):
        return (a * T + b) * D + c

    limit = 20 * 2**20 + 2 * R * (4 * half + 12 * cols)
    params = pltpu.CompilerParams(vmem_limit_bytes=limit)

    def send(block, pairs):
        return lax.ppermute(block, AXES, [(lin(*a), lin(*b)) for a, b in pairs])

    everyone = [(a, b, c) for a in range(S) for b in range(T) for c in range(D)]

    def mid(move):
        return [
            (e, move(*e) if e[2] in planes else ((e[0] + S // 2) % S, e[1], e[2])) for e in everyone
        ]

    packed = jnp.concatenate([token_ids, seg_lengths[:, :, None]], 2)
    gathered = [packed]
    for k in range(1, D):
        gathered.append(send(packed, [(e, (e[0], e[1], (e[2] + k) % D)) for e in everyone]))
    source = (z - jnp.arange(D)) % D
    chosen = (source[None, :] == jnp.arange(D)[:, None])[:, :, None, None, None]
    gathered = jnp.sum(jnp.where(chosen, jnp.stack(gathered)[None], 0), 1)
    packed = gathered.reshape(docs, segs, tokens + 1)
    ids, lengths = packed[:, :, :tokens], packed[:, :, tokens]

    def block_of(side):
        return jnp.concatenate(
            [lax.dynamic_slice_in_dim(w[0], side * cols, cols, 1) for w in (w_query, w_key, w_value)],
            1,
        )

    rounds = [c for c in range(D) if c != lo]
    blocks = [block_of((z == D - 1 - c).astype(jnp.int32)) for c in rounds]
    own_block = block_of((z == hi).astype(jnp.int32))
    where = jnp.stack([z] + [jnp.where(z == hi, D - 1 - c, c) for c in rounds]).astype(jnp.int32)

    def relay(parity, sent):
        moved = []
        for c, block in zip(rounds, sent):
            pairs = []
            for a in range(parity, S, 2):
                for b in range(T):
                    pairs.append(((a, b, c), (a, b, lo)))
                    pairs.append(((a, b, D - 1 - c), (a, b, hi)))
            moved.append(send(block, pairs))
        return moved

    vocab = emb_table.shape[0]

    def embed(index):
        local = index.reshape(-1) - s * vocab
        owned = (local >= 0) & (local < vocab)
        picked = jnp.take(emb_table, jnp.clip(local, 0, vocab - 1), axis=0)
        picked = jnp.where(owned[:, None], picked, jnp.zeros_like(picked))
        full = picked
        for a in range(1, S):
            full = full + send(picked, [((a, b, c), (0, b, c)) for b in range(T) for c in planes])
        return full, send(full, [((0, b, c), (0, T - 1 - b, c)) for b in range(T) for c in planes])

    ids, blocks = lax.optimization_barrier((ids, blocks))
    first_ids, rest_ids = ids[:n, 0], ids[n:, 0]
    later_ids = jnp.concatenate([ids[:, seg] for seg in range(1, segs)])
    even = relay(0, blocks)
    tok_first = embed(first_ids)
    mem_other = send(mem_init, [((0, b, c), (0, T - 1 - b, c)) for b in range(T) for c in planes])
    gate = sum(e[:M, :HD].astype(jnp.float32) for e in even).astype(jnp.bfloat16)
    gate = send(gate, [(e, (e[0] ^ 1, e[1], e[2])) for e in everyone])
    blocks, gate, even, tok_first, mem_other, rest_ids = lax.optimization_barrier(
        (blocks, gate, even, tok_first, mem_other, rest_ids)
    )
    odd = relay(1, blocks)
    zero = jnp.minimum(jnp.abs(gate[0, 0]), 0).astype(jnp.int32)
    tok_rest = embed(rest_ids + zero)

    offset = jnp.arange(turns) - s
    group = offset % S
    segment = jnp.clip(offset // S, 0, segs - 1)
    grouped = lengths.reshape(S, n, segs)
    lens = grouped[group, :, segment]
    active = (offset >= 0) & (offset < segs * S)
    flags = jnp.stack(
        [
            jnp.full((turns,), s == 0),
            (s == 0) & (offset < S),
            jnp.full((turns,), t),
            active & (segment == segs - 1),
        ],
        1,
    ).astype(jnp.int32)
    meta = jnp.concatenate([flags, lens], 1).astype(jnp.int32)

    shifts = [(j, i) for i in range(2) for j in range(T)]
    side = (z == hi).astype(jnp.int32)
    place = jnp.stack([((t + j) % T) * 2 + (side + i) % 2 for j, i in shifts]).astype(jnp.int32)

    smem = pl.BlockSpec(memory_space=pltpu.SMEM)
    vmem = pl.BlockSpec(memory_space=pltpu.VMEM)
    out_proj = w_out[0]
    parts = len(shifts)

    own = jnp.zeros((R, half), jnp.bfloat16)
    other = jnp.zeros((R, half), jnp.bfloat16)
    pools = []
    for k in range(turns):
        if k == 0:
            weights = [own_block] + even
            tk, tko = tok_first
        elif k == 1:
            count = len(even)
            weights = [own_block] + list(
                pl.pallas_call(
                    functools.partial(choose_kernel, count),
                    out_shape=[jax.ShapeDtypeStruct(e.shape, e.dtype) for e in even],
                    in_specs=[smem] + [pl.BlockSpec(memory_space=pl.ANY)] * (2 * count),
                    out_specs=[vmem] * count,
                    scratch_shapes=[pltpu.SemaphoreType.DMA((count,))],
                    compiler_params=params,
                )((s % 2).astype(jnp.int32).reshape(1), *even, *odd)
            )
        if k > 0:
            step = n * tokens
            at = min(k, segs * S - 1) - (1 if k < S else S)
            tk, tko = (
                a[at * step : (at + 1) * step] for a in (tok_rest if k < S else tok_later)
            )
        mixed, keep = pl.pallas_call(
            functools.partial(attend_kernel, k, n, tokens, D),
            out_shape=(
                jax.ShapeDtypeStruct((R, cols), jnp.bfloat16),
                jax.ShapeDtypeStruct((R, half), jnp.bfloat16),
            ),
            in_specs=[smem, smem] + [vmem] * (7 + len(weights)),
            out_specs=(vmem, vmem),
            scratch_shapes=[
                pltpu.VMEM((R, 2 * half), jnp.bfloat16),
                pltpu.VMEM((R, 3 * cols), jnp.float32),
            ],
            compiler_params=params,
        )(meta, where, own, other, tk, tko, mem_init, mem_other, norm_gain, *weights)
        shared = [mixed]
        if k == 0:
            later_ids, mixed = lax.optimization_barrier((later_ids, mixed))
            tok_later = embed(later_ids)
        for j, i in shifts[1:]:
            def back(a, b, c):
                return (a, (b - j) % T, planes[(planes.index(c) + i) % 2])

            shared.append(send(mixed, mid(back)))
        pool = k >= (segs - 1) * S
        shapes = [jax.ShapeDtypeStruct((R, half), jnp.bfloat16)]
        if pool:
            shapes.append(jax.ShapeDtypeStruct((n, half), jnp.float32))
        result = pl.pallas_call(
            functools.partial(project_kernel, k, n, tokens, parts, pool),
            out_shape=tuple(shapes),
            in_specs=[smem, smem, smem] + [vmem] * (parts + 2),
            out_specs=tuple([vmem] * len(shapes)),
            compiler_params=params,
        )(meta, place, layer_mix, *shared, keep, out_proj)
        if pool:
            pools.append(result[1])
        if k < turns - 1:
            own = send(result[0], [(e, ((e[0] + 1) % S, e[1], e[2])) for e in everyone])
            other = send(result[0], [(e, ((e[0] + 1) % S, T - 1 - e[1], e[2])) for e in everyone])

    mine = lax.dynamic_slice_in_dim(jnp.stack(pools), s, S, 0).reshape(docs, half)
    total = mine
    for a in range(1, S):
        total = total + send(mine, [(e, ((e[0] + a) % S, e[1], e[2])) for e in everyone])
    spread = total
    for k in range(1, D // 2):
        ends = ((lo, lo - k), (hi, hi + k))
        pairs = [((a, b, c), (a, b, e)) for a in range(S) for b in range(T) for c, e in ends]
        got = send(total, pairs + [(e, c) for c, e in pairs])
        spread = jnp.where((z == lo - k) | (z == hi + k), got, spread)
    return spread


def solution(mesh):
    return jax.shard_map(
        body,
        mesh=mesh,
        in_specs=(
            P("doc", None, None),
            P("doc", None),
            P("section", "tp"),
            P(None, "tp"),
            P("section", None),
            P("section", "doc", "tp"),
            P("section", "doc", "tp"),
            P("section", "doc", "tp"),
            P("section", None, "tp"),
            P("section"),
        ),
        out_specs=P(None, "tp"),
        check_vma=False,
    )
```

```python
import functools
import math

import jax
import jax.numpy as jnp
from jax import lax
from jax.experimental import pallas as pl
from jax.experimental.pallas import tpu as pltpu
from jax.sharding import PartitionSpec as P

HD = 128
M = 16
EPSILON = 1e-05
AXES = ("section", "tp", "doc")
C_FIRST, C_INIT, C_TP, C_POOL, C_LEN = 0, 1, 2, 3, 4


def attend_kernel(turn, docs, tokens, blocks, meta, where, *refs):
    halves = refs[0]
    other = refs[1]
    tok, tok_other, mem, mem_other, gain = refs[2:7]
    weights = refs[7 : 7 + blocks]
    mixed_ref, keep_ref = refs[7 + blocks : 9 + blocks]
    normed, acc = refs[9 + blocks :]
    rows = M + tokens
    half = halves.shape[1]
    depth = weights[0].shape[0]
    cols = weights[0].shape[1] // 3
    first = meta[turn, C_FIRST] == 1
    initial = meta[turn, C_INIT] == 1
    tp = meta[turn, C_TP]

    def prepare(doc, _):
        base = pl.multiple_of(doc * rows, 16)
        tbase = pl.multiple_of(doc * tokens, 16)
        parts = []
        for block, tk, mm in ((halves, tok, mem), (other, tok_other, mem_other)):
            head = jnp.where(initial, mm[...], block[pl.ds(base, M), :])
            body = jnp.where(
                first, tk[pl.ds(tbase, tokens), :], block[pl.ds(base + M, tokens), :]
            )
            parts.append(jnp.concatenate([head, body], 0))
        keep_ref[pl.ds(base, rows), :] = parts[0]
        floats = [p.astype(jnp.float32) for p in parts]
        square = sum(jnp.sum(f * f, -1, keepdims=True) for f in floats)
        scale = lax.rsqrt(square * (1.0 / (2 * half)) + EPSILON)
        for j, f in enumerate(floats):
            at = pl.multiple_of((tp if j == 0 else 1 - tp) * half, 128)
            normed[pl.ds(base, rows), pl.ds(at, half)] = (
                f * scale * gain[:, pl.ds(at, half)]
            ).astype(jnp.bfloat16)
        return 0

    lax.fori_loop(0, docs, prepare, 0)
    for b in range(blocks):
        at = pl.multiple_of(where[b] * depth, 128)
        left = normed[:, pl.ds(at, depth)]
        for c in range(3):
            span = pl.ds(c * cols, cols)
            part = jnp.dot(left, weights[b][:, span], preferred_element_type=jnp.float32)
            if b == 0:
                acc[:, span] = part
            else:
                acc[:, span] += part

    row = lax.broadcasted_iota(jnp.int32, (rows, rows), 0)
    col = lax.broadcasted_iota(jnp.int32, (rows, rows), 1)
    ordered = (col < M) | (row < M) | (col <= row)

    def one(doc, _):
        base = pl.multiple_of(doc * rows, 16)
        length = meta[turn, C_LEN + doc]
        allowed = ordered & ((col < M) | (col - M < length))
        for h in range(cols // HD):
            q, k, v = (
                acc[pl.ds(base, rows), c * cols + h * HD : c * cols + (h + 1) * HD].astype(
                    jnp.bfloat16
                )
                for c in range(3)
            )
            scores = lax.dot_general(
                q, k, (((1,), (1,)), ((), ())), preferred_element_type=jnp.float32
            ) * (1.0 / math.sqrt(HD))
            raw = jnp.where(allowed, jnp.exp(jnp.where(allowed, scores, -1e30)), 0.0)
            probs = (raw / jnp.sum(raw, -1, keepdims=True)).astype(jnp.bfloat16)
            mixed_ref[pl.ds(base, rows), h * HD : (h + 1) * HD] = jnp.dot(
                probs, v, preferred_element_type=jnp.float32
            ).astype(jnp.bfloat16)
        return 0

    lax.fori_loop(0, docs, one, 0)


def project_kernel(turn, docs, tokens, parts, pool, meta, place, mix, *refs):
    mixed = refs[:parts]
    keep, weight = refs[parts : parts + 2]
    outs = refs[parts + 2 :]
    if pool:
        out, pooled = outs
    else:
        (out,) = outs
    rows = M + tokens
    depth = mixed[0].shape[1]
    width = keep.shape[1]
    step = min(width, 512)
    for c in range(0, width, step):
        total = keep[:, c : c + step].astype(jnp.float32)
        for b in range(parts):
            at = pl.multiple_of(place[b] * depth, 128)
            total += jnp.dot(
                mixed[b][...],
                weight[pl.ds(at, depth), c : c + step],
                preferred_element_type=jnp.float32,
            )
        out[:, c : c + step] = total.astype(jnp.bfloat16)
    if pool:
        wanted = meta[turn, C_POOL] == 1
        place_row = lax.broadcasted_iota(jnp.int32, (rows, width), 0)
        for doc in range(docs):
            length = meta[turn, C_LEN + doc]
            ok = (place_row >= M) & (place_row - M < length) & wanted
            values = out[doc * rows : (doc + 1) * rows, :].astype(jnp.float32)
            summed = jnp.sum(jnp.where(ok, values, 0.0), 0, keepdims=True)
            pooled[doc : doc + 1, :] = summed * (mix[0] / jnp.maximum(length, 1).astype(jnp.float32))


def body(
    token_ids,
    seg_lengths,
    emb_table,
    mem_init,
    norm_gain,
    w_query,
    w_key,
    w_value,
    w_out,
    layer_mix,
):
    S, T, D = (lax.axis_size(a) for a in AXES)
    s, t, z = (lax.axis_index(a) for a in AXES)
    docs_local, segs, tokens = token_ids.shape
    docs = docs_local * D
    n = docs // S
    rows = M + tokens
    R = n * rows
    half = emb_table.shape[1]
    depth = w_query.shape[1]
    cols = w_query.shape[2] // 2
    lo, hi = D // 2 - 1, D // 2
    planes = (lo, hi)
    turns = segs * S + S - 1

    def lin(a, b, c):
        return (a * T + b) * D + c

    limit = 20 * 2**20 + 2 * R * (4 * half + 12 * cols)
    params = pltpu.CompilerParams(vmem_limit_bytes=limit)

    def send(block, pairs):
        return lax.ppermute(block, AXES, [(lin(*a), lin(*b)) for a, b in pairs])

    everyone = [(a, b, c) for a in range(S) for b in range(T) for c in range(D)]

    def mid(move):
        return [
            (e, move(*e) if e[2] in planes else ((e[0] + S // 2) % S, e[1], e[2])) for e in everyone
        ]

    packed = jnp.concatenate([token_ids, seg_lengths[:, :, None]], 2)
    gathered = [packed]
    for k in range(1, D):
        gathered.append(send(packed, [(e, (e[0], e[1], (e[2] + k) % D)) for e in everyone]))
    source = (z - jnp.arange(D)) % D
    chosen = (source[None, :] == jnp.arange(D)[:, None])[:, :, None, None, None]
    gathered = jnp.sum(jnp.where(chosen, jnp.stack(gathered)[None], 0), 1)
    packed = gathered.reshape(docs, segs, tokens + 1)
    ids, lengths = packed[:, :, :tokens], packed[:, :, tokens]

    def block_of(side):
        return jnp.concatenate(
            [lax.dynamic_slice_in_dim(w[0], side * cols, cols, 1) for w in (w_query, w_key, w_value)],
            1,
        )

    rounds = [c for c in range(D) if c != lo]
    blocks = [block_of((z == D - 1 - c).astype(jnp.int32)) for c in rounds]
    own_block = block_of((z == hi).astype(jnp.int32))
    where = jnp.stack([z] + [jnp.where(z == hi, D - 1 - c, c) for c in rounds]).astype(jnp.int32)

    def relay(c, block):
        pairs = []
        for a in range(S):
            for b in range(T):
                pairs.append(((a, b, c), (a, b, lo)))
                pairs.append(((a, b, D - 1 - c), (a, b, hi)))
        return send(block, pairs)

    vocab = emb_table.shape[0]

    def embed(index):
        local = index.reshape(-1) - s * vocab
        owned = (local >= 0) & (local < vocab)
        picked = jnp.take(emb_table, jnp.clip(local, 0, vocab - 1), axis=0)
        picked = jnp.where(owned[:, None], picked, jnp.zeros_like(picked))
        full = picked
        for a in range(1, S):
            full = full + send(picked, [((a, b, c), (0, b, c)) for b in range(T) for c in planes])
        return full, send(full, [((0, b, c), (0, T - 1 - b, c)) for b in range(T) for c in planes])

    ids, blocks = lax.optimization_barrier((ids, blocks))
    early = [relay(c, block) for c, block in zip(rounds[:-1], blocks[:-1])]
    last, early = lax.optimization_barrier((blocks[-1], early))
    weights = [own_block] + early + [relay(rounds[-1], last)]
    tok, tok_other = embed(jnp.concatenate([ids[:, seg] for seg in range(segs)]))
    mem_other = send(mem_init, [((0, b, c), (0, T - 1 - b, c)) for b in range(T) for c in planes])

    offset = jnp.arange(turns) - s
    group = offset % S
    segment = jnp.clip(offset // S, 0, segs - 1)
    grouped = lengths.reshape(S, n, segs)
    lens = grouped[group, :, segment]
    active = (offset >= 0) & (offset < segs * S)
    flags = jnp.stack(
        [
            jnp.full((turns,), s == 0),
            (s == 0) & (offset < S),
            jnp.full((turns,), t),
            active & (segment == segs - 1),
        ],
        1,
    ).astype(jnp.int32)
    meta = jnp.concatenate([flags, lens], 1).astype(jnp.int32)

    shifts = [(j, i) for i in range(2) for j in range(T)]
    side = (z == hi).astype(jnp.int32)
    place = jnp.stack([((t + j) % T) * 2 + (side + i) % 2 for j, i in shifts]).astype(jnp.int32)

    smem = pl.BlockSpec(memory_space=pltpu.SMEM)
    vmem = pl.BlockSpec(memory_space=pltpu.VMEM)
    out_proj = w_out[0]
    parts = len(shifts)

    own = jnp.zeros((R, half), jnp.bfloat16)
    other = jnp.zeros((R, half), jnp.bfloat16)
    pools = []
    for k in range(turns):
        step = n * tokens
        at = min(k, segs * S - 1) * step
        tk, tko = tok[at : at + step], tok_other[at : at + step]
        mixed, keep = pl.pallas_call(
            functools.partial(attend_kernel, k, n, tokens, D),
            out_shape=(
                jax.ShapeDtypeStruct((R, cols), jnp.bfloat16),
                jax.ShapeDtypeStruct((R, half), jnp.bfloat16),
            ),
            in_specs=[smem, smem] + [vmem] * (7 + len(weights)),
            out_specs=(vmem, vmem),
            scratch_shapes=[
                pltpu.VMEM((R, 2 * half), jnp.bfloat16),
                pltpu.VMEM((R, 3 * cols), jnp.float32),
            ],
            compiler_params=params,
        )(meta, where, own, other, tk, tko, mem_init, mem_other, norm_gain, *weights)
        shared = [mixed]
        for j, i in shifts[1:]:
            def back(a, b, c):
                return (a, (b - j) % T, planes[(planes.index(c) + i) % 2])

            shared.append(send(mixed, mid(back)))
        pool = k >= (segs - 1) * S
        shapes = [jax.ShapeDtypeStruct((R, half), jnp.bfloat16)]
        if pool:
            shapes.append(jax.ShapeDtypeStruct((n, half), jnp.float32))
        result = pl.pallas_call(
            functools.partial(project_kernel, k, n, tokens, parts, pool),
            out_shape=tuple(shapes),
            in_specs=[smem, smem, smem] + [vmem] * (parts + 2),
            out_specs=tuple([vmem] * len(shapes)),
            compiler_params=params,
        )(meta, place, layer_mix, *shared, keep, out_proj)
        if pool:
            pools.append(result[1])
        if k < turns - 1:
            own = send(result[0], [(e, ((e[0] + 1) % S, e[1], e[2])) for e in everyone])
            other = send(result[0], [(e, ((e[0] + 1) % S, T - 1 - e[1], e[2])) for e in everyone])

    mine = lax.dynamic_slice_in_dim(jnp.stack(pools), s, S, 0).reshape(docs, half)
    total = mine
    for a in range(1, S):
        total = total + send(mine, [(e, ((e[0] + a) % S, e[1], e[2])) for e in everyone])
    spread = total
    for k in range(1, D // 2):
        ends = ((lo, lo - k), (hi, hi + k))
        pairs = [((a, b, c), (a, b, e)) for a in range(S) for b in range(T) for c, e in ends]
        got = send(total, pairs + [(e, c) for c, e in pairs])
        spread = jnp.where((z == lo - k) | (z == hi + k), got, spread)
    return spread


def solution(mesh):
    return jax.shard_map(
        body,
        mesh=mesh,
        in_specs=(
            P("doc", None, None),
            P("doc", None),
            P("section", "tp"),
            P(None, "tp"),
            P("section", None),
            P("section", "doc", "tp"),
            P("section", "doc", "tp"),
            P("section", "doc", "tp"),
            P("section", None, "tp"),
            P("section"),
        ),
        out_specs=P(None, "tp"),
        check_vma=False,
    )
```

```python
import functools
import math

import jax
import jax.numpy as jnp
from jax import lax
from jax.experimental import pallas as pl
from jax.experimental.pallas import tpu as pltpu
from jax.sharding import PartitionSpec as P

HD = 128
M = 16
EPSILON = 1e-05
AXES = ("section", "tp", "doc")
C_FIRST, C_INIT, C_TP, C_POOL, C_LEN = 0, 1, 2, 3, 4


def attend_kernel(turn, docs, tokens, blocks, meta, where, *refs):
    halves = refs[0]
    other = refs[1]
    tok, tok_other, mem, mem_other, gain = refs[2:7]
    weights = refs[7 : 7 + blocks]
    mixed_ref, keep_ref = refs[7 + blocks : 9 + blocks]
    normed, acc = refs[9 + blocks :]
    rows = M + tokens
    half = halves.shape[1]
    depth = weights[0].shape[0]
    cols = weights[0].shape[1] // 3
    first = meta[turn, C_FIRST] == 1
    initial = meta[turn, C_INIT] == 1
    tp = meta[turn, C_TP]

    def prepare(doc, _):
        base = pl.multiple_of(doc * rows, 16)
        tbase = pl.multiple_of(doc * tokens, 16)
        parts = []
        for block, tk, mm in ((halves, tok, mem), (other, tok_other, mem_other)):
            head = jnp.where(initial, mm[...], block[pl.ds(base, M), :])
            body = jnp.where(
                first, tk[pl.ds(tbase, tokens), :], block[pl.ds(base + M, tokens), :]
            )
            parts.append(jnp.concatenate([head, body], 0))
        keep_ref[pl.ds(base, rows), :] = parts[0]
        floats = [p.astype(jnp.float32) for p in parts]
        square = sum(jnp.sum(f * f, -1, keepdims=True) for f in floats)
        scale = lax.rsqrt(square * (1.0 / (2 * half)) + EPSILON)
        for j, f in enumerate(floats):
            at = pl.multiple_of((tp if j == 0 else 1 - tp) * half, 128)
            normed[pl.ds(base, rows), pl.ds(at, half)] = (
                f * scale * gain[:, pl.ds(at, half)]
            ).astype(jnp.bfloat16)
        return 0

    together = docs if docs <= 4 else 1
    lax.fori_loop(0, docs, prepare, 0, unroll=together)
    for b in range(blocks):
        at = pl.multiple_of(where[b] * depth, 128)
        left = normed[:, pl.ds(at, depth)]
        for c in range(3):
            span = pl.ds(c * cols, cols)
            part = jnp.dot(left, weights[b][:, span], preferred_element_type=jnp.float32)
            if b == 0:
                acc[:, span] = part
            else:
                acc[:, span] += part

    row = lax.broadcasted_iota(jnp.int32, (rows, rows), 0)
    col = lax.broadcasted_iota(jnp.int32, (rows, rows), 1)
    ordered = (col < M) | (row < M) | (col <= row)

    def one(doc, _):
        base = pl.multiple_of(doc * rows, 16)
        length = meta[turn, C_LEN + doc]
        allowed = ordered & ((col < M) | (col - M < length))
        for h in range(cols // HD):
            q, k, v = (
                acc[pl.ds(base, rows), c * cols + h * HD : c * cols + (h + 1) * HD].astype(
                    jnp.bfloat16
                )
                for c in range(3)
            )
            scores = lax.dot_general(
                q, k, (((1,), (1,)), ((), ())), preferred_element_type=jnp.float32
            ) * (1.0 / math.sqrt(HD))
            raw = jnp.where(allowed, jnp.exp(jnp.where(allowed, scores, -1e30)), 0.0)
            probs = (raw / jnp.sum(raw, -1, keepdims=True)).astype(jnp.bfloat16)
            mixed_ref[pl.ds(base, rows), h * HD : (h + 1) * HD] = jnp.dot(
                probs, v, preferred_element_type=jnp.float32
            ).astype(jnp.bfloat16)
        return 0

    lax.fori_loop(0, docs, one, 0, unroll=together)


def hold_kernel(count, *refs):
    outs, sems = refs[count : 2 * count], refs[2 * count]
    copies = [pltpu.make_async_copy(refs[b], outs[b], sems.at[b]) for b in range(count)]
    for copy in copies:
        copy.start()
    for copy in copies:
        copy.wait()


def project_kernel(turn, docs, tokens, parts, pool, meta, place, mix, *refs):
    mixed = refs[:parts]
    keep, weight = refs[parts : parts + 2]
    outs = refs[parts + 2 :]
    if pool:
        out, pooled = outs
    else:
        (out,) = outs
    rows = M + tokens
    depth = mixed[0].shape[1]
    width = keep.shape[1]
    step = min(width, 512)
    for c in range(0, width, step):
        total = keep[:, c : c + step].astype(jnp.float32)
        for b in range(parts):
            at = pl.multiple_of(place[b] * depth, 128)
            total += jnp.dot(
                mixed[b][...],
                weight[pl.ds(at, depth), c : c + step],
                preferred_element_type=jnp.float32,
            )
        out[:, c : c + step] = total.astype(jnp.bfloat16)
    if pool:
        wanted = meta[turn, C_POOL] == 1
        place_row = lax.broadcasted_iota(jnp.int32, (rows, width), 0)
        for doc in range(docs):
            length = meta[turn, C_LEN + doc]
            ok = (place_row >= M) & (place_row - M < length) & wanted
            values = out[doc * rows : (doc + 1) * rows, :].astype(jnp.float32)
            summed = jnp.sum(jnp.where(ok, values, 0.0), 0, keepdims=True)
            pooled[doc : doc + 1, :] = summed * (mix[0] / jnp.maximum(length, 1).astype(jnp.float32))


def body(
    token_ids,
    seg_lengths,
    emb_table,
    mem_init,
    norm_gain,
    w_query,
    w_key,
    w_value,
    w_out,
    layer_mix,
):
    S, T, D = (lax.axis_size(a) for a in AXES)
    s, t, z = (lax.axis_index(a) for a in AXES)
    docs_local, segs, tokens = token_ids.shape
    docs = docs_local * D
    n = docs // S
    rows = M + tokens
    R = n * rows
    half = emb_table.shape[1]
    depth = w_query.shape[1]
    cols = w_query.shape[2] // 2
    lo, hi = D // 2 - 1, D // 2
    planes = (lo, hi)
    turns = segs * S + S - 1

    def lin(a, b, c):
        return (a * T + b) * D + c

    limit = 20 * 2**20 + 2 * R * (4 * half + 12 * cols)
    params = pltpu.CompilerParams(vmem_limit_bytes=limit)

    def send(block, pairs):
        return lax.ppermute(block, AXES, [(lin(*a), lin(*b)) for a, b in pairs])

    everyone = [(a, b, c) for a in range(S) for b in range(T) for c in range(D)]

    def mid(move):
        return [
            (e, move(*e) if e[2] in planes else ((e[0] + S // 2) % S, e[1], e[2])) for e in everyone
        ]

    packed = jnp.concatenate([token_ids, seg_lengths[:, :, None]], 2)
    gathered = [packed]
    for k in range(1, D):
        gathered.append(send(packed, [(e, (e[0], e[1], (e[2] + k) % D)) for e in everyone]))
    source = (z - jnp.arange(D)) % D
    chosen = (source[None, :] == jnp.arange(D)[:, None])[:, :, None, None, None]
    gathered = jnp.sum(jnp.where(chosen, jnp.stack(gathered)[None], 0), 1)
    packed = gathered.reshape(docs, segs, tokens + 1)
    ids, lengths = packed[:, :, :tokens], packed[:, :, tokens]

    def block_of(side):
        return jnp.concatenate(
            [lax.dynamic_slice_in_dim(w[0], side * cols, cols, 1) for w in (w_query, w_key, w_value)],
            1,
        )

    rounds = [c for c in range(D) if c != lo]
    blocks = [block_of((z == D - 1 - c).astype(jnp.int32)) for c in rounds]
    own_block = block_of((z == hi).astype(jnp.int32))
    where = jnp.stack([z] + [jnp.where(z == hi, D - 1 - c, c) for c in rounds]).astype(jnp.int32)

    def relay(c, block):
        pairs = []
        for a in range(S):
            for b in range(T):
                pairs.append(((a, b, c), (a, b, lo)))
                pairs.append(((a, b, D - 1 - c), (a, b, hi)))
        return send(block, pairs)

    vocab = emb_table.shape[0]

    def embed(index):
        local = index.reshape(-1) - s * vocab
        owned = (local >= 0) & (local < vocab)
        picked = jnp.take(emb_table, jnp.clip(local, 0, vocab - 1), axis=0)
        picked = jnp.where(owned[:, None], picked, jnp.zeros_like(picked))
        full = picked
        for a in range(1, S):
            full = full + send(picked, [((a, b, c), (0, b, c)) for b in range(T) for c in planes])
        return full, send(full, [((0, b, c), (0, T - 1 - b, c)) for b in range(T) for c in planes])

    blocks = [lax.optimization_barrier((block, ids))[0] for block in blocks]
    early = [relay(c, block) for c, block in zip(rounds[:-1], blocks[:-1])]
    last, early = lax.optimization_barrier((blocks[-1], early))
    received = early + [relay(rounds[-1], last)]
    tok, tok_other = embed(jnp.concatenate([ids[:, seg] for seg in range(segs)]))
    mem_other = send(mem_init, [((0, b, c), (0, T - 1 - b, c)) for b in range(T) for c in planes])

    offset = jnp.arange(turns) - s
    group = offset % S
    segment = jnp.clip(offset // S, 0, segs - 1)
    grouped = lengths.reshape(S, n, segs)
    lens = grouped[group, :, segment]
    active = (offset >= 0) & (offset < segs * S)
    flags = jnp.stack(
        [
            jnp.full((turns,), s == 0),
            (s == 0) & (offset < S),
            jnp.full((turns,), t),
            active & (segment == segs - 1),
        ],
        1,
    ).astype(jnp.int32)
    meta = jnp.concatenate([flags, lens], 1).astype(jnp.int32)

    shifts = [(j, i) for i in range(2) for j in range(T)]
    side = (z == hi).astype(jnp.int32)
    place = jnp.stack([((t + j) % T) * 2 + (side + i) % 2 for j, i in shifts]).astype(jnp.int32)

    smem = pl.BlockSpec(memory_space=pltpu.SMEM)
    vmem = pl.BlockSpec(memory_space=pltpu.VMEM)
    out_proj = w_out[0]
    parts = len(shifts)

    held = pl.pallas_call(
        functools.partial(hold_kernel, len(received)),
        out_shape=[jax.ShapeDtypeStruct(w.shape, w.dtype) for w in received],
        in_specs=[pl.BlockSpec(memory_space=pl.ANY)] * len(received),
        out_specs=[vmem] * len(received),
        scratch_shapes=[pltpu.SemaphoreType.DMA((len(received),))],
        compiler_params=params,
    )(*received)
    weights = [own_block, *held]

    own = jnp.zeros((R, half), jnp.bfloat16)
    other = jnp.zeros((R, half), jnp.bfloat16)
    pools = []
    for k in range(turns):
        step = n * tokens
        at = min(k, segs * S - 1) * step
        tk, tko = tok[at : at + step], tok_other[at : at + step]
        mixed, keep = pl.pallas_call(
            functools.partial(attend_kernel, k, n, tokens, D),
            out_shape=(
                jax.ShapeDtypeStruct((R, cols), jnp.bfloat16),
                jax.ShapeDtypeStruct((R, half), jnp.bfloat16),
            ),
            in_specs=[smem, smem] + [vmem] * (7 + len(weights)),
            out_specs=(vmem, vmem),
            scratch_shapes=[
                pltpu.VMEM((R, 2 * half), jnp.bfloat16),
                pltpu.VMEM((R, 3 * cols), jnp.float32),
            ],
            compiler_params=params,
        )(meta, where, own, other, tk, tko, mem_init, mem_other, norm_gain, *weights)
        shared = [mixed]
        for j, i in shifts[1:]:
            def back(a, b, c):
                return (a, (b - j) % T, planes[(planes.index(c) + i) % 2])

            shared.append(send(mixed, mid(back)))
        pool = k >= (segs - 1) * S
        shapes = [jax.ShapeDtypeStruct((R, half), jnp.bfloat16)]
        if pool:
            shapes.append(jax.ShapeDtypeStruct((n, half), jnp.float32))
        result = pl.pallas_call(
            functools.partial(project_kernel, k, n, tokens, parts, pool),
            out_shape=tuple(shapes),
            in_specs=[smem, smem, smem] + [vmem] * (parts + 2),
            out_specs=tuple([vmem] * len(shapes)),
            compiler_params=params,
        )(meta, place, layer_mix, *shared, keep, out_proj)
        if pool:
            pools.append(result[1])
        if k < turns - 1:
            paired = S % 2 == 0 and k in (0, turns - 2)
            after = [e[0] ^ 1 if paired else (e[0] + 1) % S for e in everyone]
            own = send(result[0], [(e, (a, e[1], e[2])) for e, a in zip(everyone, after)])
            other = send(result[0], [(e, (a, T - 1 - e[1], e[2])) for e, a in zip(everyone, after)])

    mine = lax.dynamic_slice_in_dim(jnp.stack(pools), s, S, 0).reshape(docs, half)
    total = mine
    for a in range(1, S):
        total = total + send(mine, [(e, ((e[0] + a) % S, e[1], e[2])) for e in everyone])
    spread = total
    for k in range(1, D // 2):
        ends = ((lo, lo - k), (hi, hi + k))
        pairs = [((a, b, c), (a, b, e)) for a in range(S) for b in range(T) for c, e in ends]
        got = send(total, pairs + [(e, c) for c, e in pairs])
        spread = jnp.where((z == lo - k) | (z == hi + k), got, spread)
    return spread


def solution(mesh):
    return jax.shard_map(
        body,
        mesh=mesh,
        in_specs=(
            P("doc", None, None),
            P("doc", None),
            P("section", "tp"),
            P(None, "tp"),
            P("section", None),
            P("section", "doc", "tp"),
            P("section", "doc", "tp"),
            P("section", "doc", "tp"),
            P("section", None, "tp"),
            P("section"),
        ),
        out_specs=P(None, "tp"),
        check_vma=False,
    )
```

```python
import functools
import math

import jax
import jax.numpy as jnp
from jax import lax
from jax.experimental import pallas as pl
from jax.experimental.pallas import tpu as pltpu
from jax.sharding import PartitionSpec as P

HD = 128
M = 16
EPSILON = 1e-05
AXES = ("section", "tp", "doc")
C_FIRST, C_INIT, C_TP, C_POOL, C_LEN = 0, 1, 2, 3, 4


def attend_kernel(turn, docs, tokens, blocks, meta, where, *refs):
    halves = refs[0]
    other = refs[1]
    tok, tok_other, mem, mem_other, gain = refs[2:7]
    weights = refs[7 : 7 + blocks]
    mixed_ref, keep_ref = refs[7 + blocks : 9 + blocks]
    normed, acc = refs[9 + blocks :]
    rows = M + tokens
    half = halves.shape[1]
    depth = weights[0].shape[0]
    cols = weights[0].shape[1] // 3
    first = meta[turn, C_FIRST] == 1
    initial = meta[turn, C_INIT] == 1
    tp = meta[turn, C_TP]

    def prepare(doc, _):
        base = pl.multiple_of(doc * rows, 16)
        tbase = pl.multiple_of(doc * tokens, 16)
        parts = []
        for block, tk, mm in ((halves, tok, mem), (other, tok_other, mem_other)):
            head = jnp.where(initial, mm[...], block[pl.ds(base, M), :])
            body = jnp.where(
                first, tk[pl.ds(tbase, tokens), :], block[pl.ds(base + M, tokens), :]
            )
            parts.append(jnp.concatenate([head, body], 0))
        keep_ref[pl.ds(base, rows), :] = parts[0]
        floats = [p.astype(jnp.float32) for p in parts]
        square = sum(jnp.sum(f * f, -1, keepdims=True) for f in floats)
        scale = lax.rsqrt(square * (1.0 / (2 * half)) + EPSILON)
        for j, f in enumerate(floats):
            at = pl.multiple_of((tp if j == 0 else 1 - tp) * half, 128)
            normed[pl.ds(base, rows), pl.ds(at, half)] = (
                f * scale * gain[:, pl.ds(at, half)]
            ).astype(jnp.bfloat16)
        return 0

    together = docs if docs <= 4 else 1
    lax.fori_loop(0, docs, prepare, 0, unroll=together)
    for b in range(blocks):
        at = pl.multiple_of(where[b] * depth, 128)
        left = normed[:, pl.ds(at, depth)]
        for c in range(3):
            span = pl.ds(c * cols, cols)
            part = jnp.dot(left, weights[b][:, span], preferred_element_type=jnp.float32)
            if b == 0:
                acc[:, span] = part
            else:
                acc[:, span] += part

    row = lax.broadcasted_iota(jnp.int32, (rows, rows), 0)
    col = lax.broadcasted_iota(jnp.int32, (rows, rows), 1)
    ordered = (col < M) | (row < M) | (col <= row)

    def one(doc, _):
        base = pl.multiple_of(doc * rows, 16)
        length = meta[turn, C_LEN + doc]
        allowed = ordered & ((col < M) | (col - M < length))
        for h in range(cols // HD):
            q, k, v = (
                acc[pl.ds(base, rows), c * cols + h * HD : c * cols + (h + 1) * HD].astype(
                    jnp.bfloat16
                )
                for c in range(3)
            )
            scores = lax.dot_general(
                q, k, (((1,), (1,)), ((), ())), preferred_element_type=jnp.float32
            ) * (1.0 / math.sqrt(HD))
            raw = jnp.where(allowed, jnp.exp(jnp.where(allowed, scores, -1e30)), 0.0)
            probs = (raw / jnp.sum(raw, -1, keepdims=True)).astype(jnp.bfloat16)
            mixed_ref[pl.ds(base, rows), h * HD : (h + 1) * HD] = jnp.dot(
                probs, v, preferred_element_type=jnp.float32
            ).astype(jnp.bfloat16)
        return 0

    lax.fori_loop(0, docs, one, 0, unroll=together)


def hold_kernel(count, *refs):
    outs, sems = refs[count : 2 * count], refs[2 * count]
    copies = [pltpu.make_async_copy(refs[b], outs[b], sems.at[b]) for b in range(count)]
    for copy in copies:
        copy.start()
    for copy in copies:
        copy.wait()


def cut_kernel(count, sides, *refs):
    outs, sems = refs[3 : 3 + count], refs[3 + count]
    cols = outs[0].shape[1] // 3
    copies = []
    for b in range(count):
        at = pl.multiple_of(sides[b] * cols, 128)
        for c in range(3):
            copies.append(
                pltpu.make_async_copy(
                    refs[c].at[0, :, pl.ds(at, cols)],
                    outs[b].at[:, pl.ds(c * cols, cols)],
                    sems.at[3 * b + c],
                )
            )
    for copy in copies:
        copy.start()
    for copy in copies:
        copy.wait()


def project_kernel(turn, docs, tokens, parts, pool, meta, place, mix, *refs):
    mixed = refs[:parts]
    keep, weight = refs[parts : parts + 2]
    outs = refs[parts + 2 :]
    if pool:
        out, pooled = outs
    else:
        (out,) = outs
    rows = M + tokens
    depth = mixed[0].shape[1]
    width = keep.shape[1]
    step = min(width, 512)
    for c in range(0, width, step):
        total = keep[:, c : c + step].astype(jnp.float32)
        for b in range(parts):
            at = pl.multiple_of(place[b] * depth, 128)
            total += jnp.dot(
                mixed[b][...],
                weight[pl.ds(at, depth), c : c + step],
                preferred_element_type=jnp.float32,
            )
        out[:, c : c + step] = total.astype(jnp.bfloat16)
    if pool:
        wanted = meta[turn, C_POOL] == 1
        place_row = lax.broadcasted_iota(jnp.int32, (rows, width), 0)
        for doc in range(docs):
            length = meta[turn, C_LEN + doc]
            ok = (place_row >= M) & (place_row - M < length) & wanted
            values = out[doc * rows : (doc + 1) * rows, :].astype(jnp.float32)
            summed = jnp.sum(jnp.where(ok, values, 0.0), 0, keepdims=True)
            pooled[doc : doc + 1, :] = summed * (mix[0] / jnp.maximum(length, 1).astype(jnp.float32))


def body(
    token_ids,
    seg_lengths,
    emb_table,
    mem_init,
    norm_gain,
    w_query,
    w_key,
    w_value,
    w_out,
    layer_mix,
):
    S, T, D = (lax.axis_size(a) for a in AXES)
    s, t, z = (lax.axis_index(a) for a in AXES)
    docs_local, segs, tokens = token_ids.shape
    docs = docs_local * D
    n = docs // S
    rows = M + tokens
    R = n * rows
    half = emb_table.shape[1]
    depth = w_query.shape[1]
    cols = w_query.shape[2] // 2
    lo, hi = D // 2 - 1, D // 2
    planes = (lo, hi)
    turns = segs * S + S - 1

    def lin(a, b, c):
        return (a * T + b) * D + c

    limit = 20 * 2**20 + 2 * R * (4 * half + 12 * cols)
    params = pltpu.CompilerParams(vmem_limit_bytes=limit)

    def send(block, pairs):
        return lax.ppermute(block, AXES, [(lin(*a), lin(*b)) for a, b in pairs])

    everyone = [(a, b, c) for a in range(S) for b in range(T) for c in range(D)]

    def mid(move):
        return [
            (e, move(*e) if e[2] in planes else ((e[0] + S // 2) % S, e[1], e[2])) for e in everyone
        ]

    packed = jnp.concatenate([token_ids, seg_lengths[:, :, None]], 2)
    gathered = [packed]
    for k in range(1, D):
        gathered.append(send(packed, [(e, (e[0], e[1], (e[2] + k) % D)) for e in everyone]))
    source = (z - jnp.arange(D)) % D
    chosen = (source[None, :] == jnp.arange(D)[:, None])[:, :, None, None, None]
    gathered = jnp.sum(jnp.where(chosen, jnp.stack(gathered)[None], 0), 1)
    packed = gathered.reshape(docs, segs, tokens + 1)
    ids, lengths = packed[:, :, :tokens], packed[:, :, tokens]

    smem = pl.BlockSpec(memory_space=pltpu.SMEM)
    vmem = pl.BlockSpec(memory_space=pltpu.VMEM)
    hbm = pl.BlockSpec(memory_space=pl.ANY)

    def cut(sides):
        count = len(sides)
        size = count * depth * 3 * cols * 4
        return pl.pallas_call(
            functools.partial(cut_kernel, count),
            out_shape=[jax.ShapeDtypeStruct((depth, 3 * cols), jnp.bfloat16)] * count,
            in_specs=[smem] + [hbm] * 3,
            out_specs=[hbm] * count,
            scratch_shapes=[pltpu.SemaphoreType.DMA((3 * count,))],
            cost_estimate=pl.CostEstimate(flops=0, bytes_accessed=size, transcendentals=0),
        )(jnp.stack(sides).astype(jnp.int32), w_query, w_key, w_value)

    rounds = [c for c in range(D) if c != lo]
    blocks = list(cut([z == D - 1 - c for c in rounds[:-1]]))
    last, own_block = cut([z == D - 1 - rounds[-1], z == hi])
    blocks.append(last)
    where = jnp.stack([z] + [jnp.where(z == hi, D - 1 - c, c) for c in rounds]).astype(jnp.int32)

    def relay(c, block):
        pairs = []
        for a in range(S):
            for b in range(T):
                pairs.append(((a, b, c), (a, b, lo)))
                pairs.append(((a, b, D - 1 - c), (a, b, hi)))
        return send(block, pairs)

    vocab = emb_table.shape[0]

    def embed(index):
        local = index.reshape(-1) - s * vocab
        owned = (local >= 0) & (local < vocab)
        picked = jnp.take(emb_table, jnp.clip(local, 0, vocab - 1), axis=0)
        picked = jnp.where(owned[:, None], picked, jnp.zeros_like(picked))
        full = picked
        for a in range(1, S):
            full = full + send(picked, [((a, b, c), (0, b, c)) for b in range(T) for c in planes])
        return full, send(full, [((0, b, c), (0, T - 1 - b, c)) for b in range(T) for c in planes])

    blocks = [lax.optimization_barrier((block, ids))[0] for block in blocks]
    early = [relay(c, block) for c, block in zip(rounds[:-1], blocks[:-1])]
    last, early = lax.optimization_barrier((blocks[-1], early))
    received = [own_block] + early + [relay(rounds[-1], last)]
    tok, tok_other = embed(jnp.concatenate([ids[:, seg] for seg in range(segs)]))
    mem_other = send(mem_init, [((0, b, c), (0, T - 1 - b, c)) for b in range(T) for c in planes])

    offset = jnp.arange(turns) - s
    group = offset % S
    segment = jnp.clip(offset // S, 0, segs - 1)
    grouped = lengths.reshape(S, n, segs)
    lens = grouped[group, :, segment]
    active = (offset >= 0) & (offset < segs * S)
    flags = jnp.stack(
        [
            jnp.full((turns,), s == 0),
            (s == 0) & (offset < S),
            jnp.full((turns,), t),
            active & (segment == segs - 1),
        ],
        1,
    ).astype(jnp.int32)
    meta = jnp.concatenate([flags, lens], 1).astype(jnp.int32)

    shifts = [(j, i) for i in range(2) for j in range(T)]
    side = (z == hi).astype(jnp.int32)
    place = jnp.stack([((t + j) % T) * 2 + (side + i) % 2 for j, i in shifts]).astype(jnp.int32)

    out_proj = w_out[0]
    parts = len(shifts)

    weights = pl.pallas_call(
        functools.partial(hold_kernel, len(received)),
        out_shape=[jax.ShapeDtypeStruct(w.shape, w.dtype) for w in received],
        in_specs=[pl.BlockSpec(memory_space=pl.ANY)] * len(received),
        out_specs=[vmem] * len(received),
        scratch_shapes=[pltpu.SemaphoreType.DMA((len(received),))],
        compiler_params=params,
    )(*received)

    own = jnp.zeros((R, half), jnp.bfloat16)
    other = jnp.zeros((R, half), jnp.bfloat16)
    pools = []
    for k in range(turns):
        step = n * tokens
        at = min(k, segs * S - 1) * step
        tk, tko = tok[at : at + step], tok_other[at : at + step]
        mixed, keep = pl.pallas_call(
            functools.partial(attend_kernel, k, n, tokens, D),
            out_shape=(
                jax.ShapeDtypeStruct((R, cols), jnp.bfloat16),
                jax.ShapeDtypeStruct((R, half), jnp.bfloat16),
            ),
            in_specs=[smem, smem] + [vmem] * (7 + len(weights)),
            out_specs=(vmem, vmem),
            scratch_shapes=[
                pltpu.VMEM((R, 2 * half), jnp.bfloat16),
                pltpu.VMEM((R, 3 * cols), jnp.float32),
            ],
            compiler_params=params,
        )(meta, where, own, other, tk, tko, mem_init, mem_other, norm_gain, *weights)
        shared = [mixed]
        for j, i in shifts[1:]:
            def back(a, b, c):
                return (a, (b - j) % T, planes[(planes.index(c) + i) % 2])

            shared.append(send(mixed, mid(back)))
        pool = k >= (segs - 1) * S
        shapes = [jax.ShapeDtypeStruct((R, half), jnp.bfloat16)]
        if pool:
            shapes.append(jax.ShapeDtypeStruct((n, half), jnp.float32))
        result = pl.pallas_call(
            functools.partial(project_kernel, k, n, tokens, parts, pool),
            out_shape=tuple(shapes),
            in_specs=[smem, smem, smem] + [vmem] * (parts + 2),
            out_specs=tuple([vmem] * len(shapes)),
            compiler_params=params,
        )(meta, place, layer_mix, *shared, keep, out_proj)
        if pool:
            pools.append(result[1])
        if k < turns - 1:
            paired = S % 2 == 0 and k in (0, turns - 2)
            after = [e[0] ^ 1 if paired else (e[0] + 1) % S for e in everyone]
            own = send(result[0], [(e, (a, e[1], e[2])) for e, a in zip(everyone, after)])
            counts = {0: (0,), turns - 2: (S - 2,)}.get(k, range(S)) if paired else range(S)
            other = send(
                result[0],
                [
                    (e, (a, T - 1 - e[1] if e[0] in counts else e[1], e[2]))
                    for e, a in zip(everyone, after)
                ],
            )

    mine = lax.dynamic_slice_in_dim(jnp.stack(pools), s, S, 0).reshape(docs, half)
    total = mine
    for a in range(1, S):
        total = total + send(mine, [(e, ((e[0] + a) % S, e[1], e[2])) for e in everyone])
    spread = total
    for k in range(1, D // 2):
        ends = ((lo, lo - k), (hi, hi + k))
        pairs = [((a, b, c), (a, b, e)) for a in range(S) for b in range(T) for c, e in ends]
        got = send(total, pairs + [(e, c) for c, e in pairs])
        spread = jnp.where((z == lo - k) | (z == hi + k), got, spread)
    return spread


def solution(mesh):
    return jax.shard_map(
        body,
        mesh=mesh,
        in_specs=(
            P("doc", None, None),
            P("doc", None),
            P("section", "tp"),
            P(None, "tp"),
            P("section", None),
            P("section", "doc", "tp"),
            P("section", "doc", "tp"),
            P("section", "doc", "tp"),
            P("section", None, "tp"),
            P("section"),
        ),
        out_specs=P(None, "tp"),
        check_vma=False,
    )
```

```python
import functools
import math

import jax
import jax.numpy as jnp
from jax import lax
from jax.experimental import pallas as pl
from jax.experimental.pallas import tpu as pltpu
from jax.sharding import PartitionSpec as P

HD = 128
M = 16
EPSILON = 1e-05
AXES = ("section", "tp", "doc")
C_FIRST, C_INIT, C_TP, C_POOL, C_LEN = 0, 1, 2, 3, 4


def attend_kernel(turn, docs, tokens, blocks, meta, where, *refs):
    halves = refs[0]
    other = refs[1]
    tok, tok_other, mem, mem_other, gain = refs[2:7]
    weights = refs[7 : 7 + blocks]
    mixed_ref, keep_ref = refs[7 + blocks : 9 + blocks]
    normed, acc = refs[9 + blocks :]
    rows = M + tokens
    half = halves.shape[1]
    depth = weights[0].shape[0]
    cols = weights[0].shape[1] // 3
    first = meta[turn, C_FIRST] == 1
    initial = meta[turn, C_INIT] == 1
    tp = meta[turn, C_TP]

    def prepare(doc, _):
        base = pl.multiple_of(doc * rows, 16)
        tbase = pl.multiple_of(doc * tokens, 16)
        parts = []
        for block, tk, mm in ((halves, tok, mem), (other, tok_other, mem_other)):
            head = jnp.where(initial, mm[...], block[pl.ds(base, M), :])
            body = jnp.where(
                first, tk[pl.ds(tbase, tokens), :], block[pl.ds(base + M, tokens), :]
            )
            parts.append(jnp.concatenate([head, body], 0))
        keep_ref[pl.ds(base, rows), :] = parts[0]
        floats = [p.astype(jnp.float32) for p in parts]
        square = sum(jnp.sum(f * f, -1, keepdims=True) for f in floats)
        scale = lax.rsqrt(square * (1.0 / (2 * half)) + EPSILON)
        for j, f in enumerate(floats):
            at = pl.multiple_of((tp if j == 0 else 1 - tp) * half, 128)
            normed[pl.ds(base, rows), pl.ds(at, half)] = (
                f * scale * gain[:, pl.ds(at, half)]
            ).astype(jnp.bfloat16)
        return 0

    together = docs if docs <= 4 else 1
    lax.fori_loop(0, docs, prepare, 0, unroll=together)
    for b in range(blocks):
        at = pl.multiple_of(where[b] * depth, 128)
        left = normed[:, pl.ds(at, depth)]
        for c in range(3):
            span = pl.ds(c * cols, cols)
            part = jnp.dot(left, weights[b][:, span], preferred_element_type=jnp.float32)
            if b == 0:
                acc[:, span] = part
            else:
                acc[:, span] += part

    row = lax.broadcasted_iota(jnp.int32, (rows, rows), 0)
    col = lax.broadcasted_iota(jnp.int32, (rows, rows), 1)
    ordered = (col < M) | (row < M) | (col <= row)

    def one(doc, _):
        base = pl.multiple_of(doc * rows, 16)
        length = meta[turn, C_LEN + doc]
        allowed = ordered & ((col < M) | (col - M < length))
        for h in range(cols // HD):
            q, k, v = (
                acc[pl.ds(base, rows), c * cols + h * HD : c * cols + (h + 1) * HD].astype(
                    jnp.bfloat16
                )
                for c in range(3)
            )
            scores = lax.dot_general(
                q, k, (((1,), (1,)), ((), ())), preferred_element_type=jnp.float32
            ) * (1.0 / math.sqrt(HD))
            raw = jnp.where(allowed, jnp.exp(jnp.where(allowed, scores, -1e30)), 0.0)
            probs = (raw / jnp.sum(raw, -1, keepdims=True)).astype(jnp.bfloat16)
            mixed_ref[pl.ds(base, rows), h * HD : (h + 1) * HD] = jnp.dot(
                probs, v, preferred_element_type=jnp.float32
            ).astype(jnp.bfloat16)
        return 0

    lax.fori_loop(0, docs, one, 0, unroll=together)


def hold_kernel(count, *refs):
    outs, sems = refs[count : 2 * count], refs[2 * count]
    copies = [pltpu.make_async_copy(refs[b], outs[b], sems.at[b]) for b in range(count)]
    for copy in copies:
        copy.start()
    for copy in copies:
        copy.wait()


def project_kernel(turn, docs, tokens, parts, pool, meta, place, mix, *refs):
    mixed = refs[:parts]
    keep, weight = refs[parts : parts + 2]
    outs = refs[parts + 2 :]
    if pool:
        out, pooled = outs
    else:
        (out,) = outs
    rows = M + tokens
    depth = mixed[0].shape[1]
    width = keep.shape[1]
    step = min(width, 512)
    for c in range(0, width, step):
        total = keep[:, c : c + step].astype(jnp.float32)
        for b in range(parts):
            at = pl.multiple_of(place[b] * depth, 128)
            total += jnp.dot(
                mixed[b][...],
                weight[pl.ds(at, depth), c : c + step],
                preferred_element_type=jnp.float32,
            )
        out[:, c : c + step] = total.astype(jnp.bfloat16)
    if pool:
        wanted = meta[turn, C_POOL] == 1
        place_row = lax.broadcasted_iota(jnp.int32, (rows, width), 0)
        for doc in range(docs):
            length = meta[turn, C_LEN + doc]
            ok = (place_row >= M) & (place_row - M < length) & wanted
            values = out[doc * rows : (doc + 1) * rows, :].astype(jnp.float32)
            summed = jnp.sum(jnp.where(ok, values, 0.0), 0, keepdims=True)
            pooled[doc : doc + 1, :] = summed * (mix[0] / jnp.maximum(length, 1).astype(jnp.float32))


def body(
    token_ids,
    seg_lengths,
    emb_table,
    mem_init,
    norm_gain,
    w_query,
    w_key,
    w_value,
    w_out,
    layer_mix,
):
    S, T, D = (lax.axis_size(a) for a in AXES)
    s, t, z = (lax.axis_index(a) for a in AXES)
    docs_local, segs, tokens = token_ids.shape
    docs = docs_local * D
    n = docs // S
    rows = M + tokens
    R = n * rows
    half = emb_table.shape[1]
    depth = w_query.shape[1]
    cols = w_query.shape[2] // 2
    lo, hi = D // 2 - 1, D // 2
    planes = (lo, hi)
    turns = segs * S + S - 1

    def lin(a, b, c):
        return (a * T + b) * D + c

    limit = 20 * 2**20 + 2 * R * (4 * half + 12 * cols)
    params = pltpu.CompilerParams(vmem_limit_bytes=limit)

    def send(block, pairs):
        return lax.ppermute(block, AXES, [(lin(*a), lin(*b)) for a, b in pairs])

    everyone = [(a, b, c) for a in range(S) for b in range(T) for c in range(D)]

    def mid(move):
        return [
            (e, move(*e) if e[2] in planes else ((e[0] + S // 2) % S, e[1], e[2])) for e in everyone
        ]

    packed = jnp.concatenate([token_ids, seg_lengths[:, :, None]], 2)
    gathered = [packed]
    for k in range(1, D):
        gathered.append(send(packed, [(e, (e[0], e[1], (e[2] + k) % D)) for e in everyone]))
    source = (z - jnp.arange(D)) % D
    chosen = (source[None, :] == jnp.arange(D)[:, None])[:, :, None, None, None]
    gathered = jnp.sum(jnp.where(chosen, jnp.stack(gathered)[None], 0), 1)
    packed = gathered.reshape(docs, segs, tokens + 1)
    ids, lengths = packed[:, :, :tokens], packed[:, :, tokens]

    def block_of(side):
        return jnp.concatenate(
            [lax.dynamic_slice_in_dim(w[0], side * cols, cols, 1) for w in (w_query, w_key, w_value)],
            1,
        )

    rounds = [c for c in range(D) if c != lo]
    blocks = [block_of((z == D - 1 - c).astype(jnp.int32)) for c in rounds]
    own_block = block_of((z == hi).astype(jnp.int32))
    where = jnp.stack([z] + [jnp.where(z == hi, D - 1 - c, c) for c in rounds]).astype(jnp.int32)

    def relay(c, block):
        pairs = []
        for a in range(S):
            for b in range(T):
                pairs.append(((a, b, c), (a, b, lo)))
                pairs.append(((a, b, D - 1 - c), (a, b, hi)))
        return send(block, pairs)

    vocab = emb_table.shape[0]

    def embed(index):
        local = index.reshape(-1) - s * vocab
        owned = (local >= 0) & (local < vocab)
        picked = jnp.take(emb_table, jnp.clip(local, 0, vocab - 1), axis=0)
        picked = jnp.where(owned[:, None], picked, jnp.zeros_like(picked))
        full = picked
        for a in range(1, S):
            full = full + send(picked, [((a, b, c), (0, b, c)) for b in range(T) for c in planes])
        return full, send(full, [((0, b, c), (0, T - 1 - b, c)) for b in range(T) for c in planes])

    blocks = [lax.optimization_barrier((block, ids))[0] for block in blocks]
    early = [relay(c, block) for c, block in zip(rounds[:-1], blocks[:-1])]
    last, early = lax.optimization_barrier((blocks[-1], early))
    received = early + [relay(rounds[-1], last)]
    tok, tok_other = embed(jnp.concatenate([ids[:, seg] for seg in range(segs)]))
    mem_other = send(mem_init, [((0, b, c), (0, T - 1 - b, c)) for b in range(T) for c in planes])

    offset = jnp.arange(turns) - s
    group = offset % S
    segment = jnp.clip(offset // S, 0, segs - 1)
    grouped = lengths.reshape(S, n, segs)
    lens = grouped[group, :, segment]
    active = (offset >= 0) & (offset < segs * S)
    flags = jnp.stack(
        [
            jnp.full((turns,), s == 0),
            (s == 0) & (offset < S),
            jnp.full((turns,), t),
            active & (segment == segs - 1),
        ],
        1,
    ).astype(jnp.int32)
    meta = jnp.concatenate([flags, lens], 1).astype(jnp.int32)

    shifts = [(j, i) for i in range(2) for j in range(T)]
    side = (z == hi).astype(jnp.int32)
    place = jnp.stack([((t + j) % T) * 2 + (side + i) % 2 for j, i in shifts]).astype(jnp.int32)

    smem = pl.BlockSpec(memory_space=pltpu.SMEM)
    vmem = pl.BlockSpec(memory_space=pltpu.VMEM)
    out_proj = w_out[0]
    parts = len(shifts)

    held = pl.pallas_call(
        functools.partial(hold_kernel, len(received)),
        out_shape=[jax.ShapeDtypeStruct(w.shape, w.dtype) for w in received],
        in_specs=[pl.BlockSpec(memory_space=pl.ANY)] * len(received),
        out_specs=[vmem] * len(received),
        scratch_shapes=[pltpu.SemaphoreType.DMA((len(received),))],
        compiler_params=params,
    )(*received)
    weights = [own_block, *held]

    own = jnp.zeros((R, half), jnp.bfloat16)
    other = jnp.zeros((R, half), jnp.bfloat16)
    pools = []
    for k in range(turns):
        step = n * tokens
        at = min(k, segs * S - 1) * step
        tk, tko = tok[at : at + step], tok_other[at : at + step]
        mixed, keep = pl.pallas_call(
            functools.partial(attend_kernel, k, n, tokens, D),
            out_shape=(
                jax.ShapeDtypeStruct((R, cols), jnp.bfloat16),
                jax.ShapeDtypeStruct((R, half), jnp.bfloat16),
            ),
            in_specs=[smem, smem] + [vmem] * (7 + len(weights)),
            out_specs=(vmem, vmem),
            scratch_shapes=[
                pltpu.VMEM((R, 2 * half), jnp.bfloat16),
                pltpu.VMEM((R, 3 * cols), jnp.float32),
            ],
            compiler_params=params,
        )(meta, where, own, other, tk, tko, mem_init, mem_other, norm_gain, *weights)
        shared = [mixed]
        for j, i in shifts[1:]:
            def back(a, b, c):
                return (a, (b - j) % T, planes[(planes.index(c) + i) % 2])

            shared.append(send(mixed, mid(back)))
        pool = k >= (segs - 1) * S
        shapes = [jax.ShapeDtypeStruct((R, half), jnp.bfloat16)]
        if pool:
            shapes.append(jax.ShapeDtypeStruct((n, half), jnp.float32))
        result = pl.pallas_call(
            functools.partial(project_kernel, k, n, tokens, parts, pool),
            out_shape=tuple(shapes),
            in_specs=[smem, smem, smem] + [vmem] * (parts + 2),
            out_specs=tuple([vmem] * len(shapes)),
            compiler_params=params,
        )(meta, place, layer_mix, *shared, keep, out_proj)
        if pool:
            pools.append(result[1])
        if k < turns - 1:
            paired = S % 2 == 0 and k in (0, turns - 2)
            after = [e[0] ^ 1 if paired else (e[0] + 1) % S for e in everyone]
            own = send(result[0], [(e, (a, e[1], e[2])) for e, a in zip(everyone, after)])
            counts = {0: (0,), turns - 2: (S - 2,)}.get(k, range(S)) if paired else range(S)
            other = send(
                result[0],
                [
                    (e, (a, T - 1 - e[1] if e[0] in counts else e[1], e[2]))
                    for e, a in zip(everyone, after)
                ],
            )

    mine = lax.dynamic_slice_in_dim(jnp.stack(pools), s, S, 0).reshape(docs, half)
    total = mine
    for a in range(1, S):
        total = total + send(mine, [(e, ((e[0] + a) % S, e[1], e[2])) for e in everyone])
    spread = total
    for k in range(1, D // 2):
        ends = ((lo, lo - k), (hi, hi + k))
        pairs = [((a, b, c), (a, b, e)) for a in range(S) for b in range(T) for c, e in ends]
        got = send(total, pairs + [(e, c) for c, e in pairs])
        spread = jnp.where((z == lo - k) | (z == hi + k), got, spread)
    return spread


def solution(mesh):
    return jax.shard_map(
        body,
        mesh=mesh,
        in_specs=(
            P("doc", None, None),
            P("doc", None),
            P("section", "tp"),
            P(None, "tp"),
            P("section", None),
            P("section", "doc", "tp"),
            P("section", "doc", "tp"),
            P("section", "doc", "tp"),
            P("section", None, "tp"),
            P("section"),
        ),
        out_specs=P(None, "tp"),
        check_vma=False,
    )
```

```python
import functools
import math

import jax
import jax.numpy as jnp
from jax import lax
from jax.experimental import pallas as pl
from jax.experimental.pallas import tpu as pltpu
from jax.sharding import PartitionSpec as P

HD = 128
M = 16
EPSILON = 1e-05
AXES = ("section", "tp", "doc")
C_FIRST, C_INIT, C_TP, C_POOL, C_LEN = 0, 1, 2, 3, 4


def attend_kernel(turn, docs, tokens, blocks, meta, where, *refs):
    halves = refs[0]
    other = refs[1]
    tok, tok_other, mem, mem_other, gain = refs[2:7]
    weights = refs[7 : 7 + blocks]
    mixed_ref, keep_ref = refs[7 + blocks : 9 + blocks]
    normed, acc = refs[9 + blocks :]
    rows = M + tokens
    half = halves.shape[1]
    depth = weights[0].shape[0]
    cols = weights[0].shape[1] // 3
    first = meta[turn, C_FIRST] == 1
    initial = meta[turn, C_INIT] == 1
    tp = meta[turn, C_TP]

    def prepare(doc, _):
        base = pl.multiple_of(doc * rows, 16)
        tbase = pl.multiple_of(doc * tokens, 16)
        parts = []
        for block, tk, mm in ((halves, tok, mem), (other, tok_other, mem_other)):
            head = jnp.where(initial, mm[...], block[pl.ds(base, M), :])
            body = jnp.where(
                first, tk[pl.ds(tbase, tokens), :], block[pl.ds(base + M, tokens), :]
            )
            parts.append(jnp.concatenate([head, body], 0))
        keep_ref[pl.ds(base, rows), :] = parts[0]
        floats = [p.astype(jnp.float32) for p in parts]
        square = sum(jnp.sum(f * f, -1, keepdims=True) for f in floats)
        scale = lax.rsqrt(square * (1.0 / (2 * half)) + EPSILON)
        for j, f in enumerate(floats):
            at = pl.multiple_of((tp if j == 0 else 1 - tp) * half, 128)
            normed[pl.ds(base, rows), pl.ds(at, half)] = (
                f * scale * gain[:, pl.ds(at, half)]
            ).astype(jnp.bfloat16)
        return 0

    together = docs if docs <= 4 else 1
    lax.fori_loop(0, docs, prepare, 0, unroll=together)
    for b in range(blocks):
        at = pl.multiple_of(where[b] * depth, 128)
        left = normed[:, pl.ds(at, depth)]
        for c in range(3):
            span = pl.ds(c * cols, cols)
            part = jnp.dot(left, weights[b][:, span], preferred_element_type=jnp.float32)
            if b == 0:
                acc[:, span] = part
            else:
                acc[:, span] += part

    row = lax.broadcasted_iota(jnp.int32, (rows, rows), 0)
    col = lax.broadcasted_iota(jnp.int32, (rows, rows), 1)
    ordered = (col < M) | (row < M) | (col <= row)

    def one(doc, _):
        base = pl.multiple_of(doc * rows, 16)
        length = meta[turn, C_LEN + doc]
        allowed = ordered & ((col < M) | (col - M < length))
        for h in range(cols // HD):
            q, k, v = (
                acc[pl.ds(base, rows), c * cols + h * HD : c * cols + (h + 1) * HD].astype(
                    jnp.bfloat16
                )
                for c in range(3)
            )
            scores = lax.dot_general(
                q, k, (((1,), (1,)), ((), ())), preferred_element_type=jnp.float32
            ) * (1.0 / math.sqrt(HD))
            raw = jnp.where(allowed, jnp.exp(jnp.where(allowed, scores, -1e30)), 0.0)
            probs = (raw / jnp.sum(raw, -1, keepdims=True)).astype(jnp.bfloat16)
            mixed_ref[pl.ds(base, rows), h * HD : (h + 1) * HD] = jnp.dot(
                probs, v, preferred_element_type=jnp.float32
            ).astype(jnp.bfloat16)
        return 0

    lax.fori_loop(0, docs, one, 0, unroll=together)


def hold_kernel(count, *refs):
    outs, sems = refs[count : 2 * count], refs[2 * count]
    copies = [pltpu.make_async_copy(refs[b], outs[b], sems.at[b]) for b in range(count)]
    for copy in copies:
        copy.start()
    for copy in copies:
        copy.wait()


def project_kernel(turn, docs, tokens, parts, pool, meta, place, mix, *refs):
    mixed = refs[:parts]
    keep, weight = refs[parts : parts + 2]
    outs = refs[parts + 2 :]
    if pool:
        out, pooled = outs
    else:
        (out,) = outs
    rows = M + tokens
    depth = mixed[0].shape[1]
    width = keep.shape[1]
    step = min(width, 512)
    for c in range(0, width, step):
        total = keep[:, c : c + step].astype(jnp.float32)
        for b in range(parts):
            at = pl.multiple_of(place[b] * depth, 128)
            total += jnp.dot(
                mixed[b][...],
                weight[pl.ds(at, depth), c : c + step],
                preferred_element_type=jnp.float32,
            )
        out[:, c : c + step] = total.astype(jnp.bfloat16)
    if pool:
        wanted = meta[turn, C_POOL] == 1
        place_row = lax.broadcasted_iota(jnp.int32, (rows, width), 0)
        for doc in range(docs):
            length = meta[turn, C_LEN + doc]
            ok = (place_row >= M) & (place_row - M < length) & wanted
            values = out[doc * rows : (doc + 1) * rows, :].astype(jnp.float32)
            summed = jnp.sum(jnp.where(ok, values, 0.0), 0, keepdims=True)
            pooled[doc : doc + 1, :] = summed * (mix[0] / jnp.maximum(length, 1).astype(jnp.float32))


def body(
    token_ids,
    seg_lengths,
    emb_table,
    mem_init,
    norm_gain,
    w_query,
    w_key,
    w_value,
    w_out,
    layer_mix,
):
    S, T, D = (lax.axis_size(a) for a in AXES)
    s, t, z = (lax.axis_index(a) for a in AXES)
    docs_local, segs, tokens = token_ids.shape
    docs = docs_local * D
    n = docs // S
    rows = M + tokens
    R = n * rows
    half = emb_table.shape[1]
    depth = w_query.shape[1]
    cols = w_query.shape[2] // 2
    lo, hi = D // 2 - 1, D // 2
    planes = (lo, hi)
    turns = segs * S + S - 1

    def lin(a, b, c):
        return (a * T + b) * D + c

    limit = 20 * 2**20 + 2 * R * (4 * half + 12 * cols)
    params = pltpu.CompilerParams(vmem_limit_bytes=limit)

    def send(block, pairs):
        return lax.ppermute(block, AXES, [(lin(*a), lin(*b)) for a, b in pairs])

    everyone = [(a, b, c) for a in range(S) for b in range(T) for c in range(D)]

    def mid(move):
        return [
            (e, move(*e) if e[2] in planes else ((e[0] + S // 2) % S, e[1], e[2])) for e in everyone
        ]

    packed = jnp.concatenate([token_ids, seg_lengths[:, :, None]], 2)
    gathered = [packed]
    for k in range(1, D):
        gathered.append(send(packed, [(e, (e[0], e[1], (e[2] + k) % D)) for e in everyone]))
    source = (z - jnp.arange(D)) % D
    chosen = (source[None, :] == jnp.arange(D)[:, None])[:, :, None, None, None]
    gathered = jnp.sum(jnp.where(chosen, jnp.stack(gathered)[None], 0), 1)
    packed = gathered.reshape(docs, segs, tokens + 1)
    ids, lengths = packed[:, :, :tokens], packed[:, :, tokens]

    def block_of(side):
        return jnp.concatenate(
            [lax.dynamic_slice_in_dim(w[0], side * cols, cols, 1) for w in (w_query, w_key, w_value)],
            1,
        )

    rounds = [c for c in range(D) if c != lo]
    blocks = [block_of((z == D - 1 - c).astype(jnp.int32)) for c in rounds]
    own_block = block_of((z == hi).astype(jnp.int32))
    where = jnp.stack([z] + [jnp.where(z == hi, D - 1 - c, c) for c in rounds]).astype(jnp.int32)

    def relay(c, block):
        pairs = []
        for a in range(S):
            for b in range(T):
                pairs.append(((a, b, c), (a, b, lo)))
                pairs.append(((a, b, D - 1 - c), (a, b, hi)))
        return send(block, pairs)

    vocab = emb_table.shape[0]

    def embed(index):
        local = index.reshape(-1) - s * vocab
        owned = (local >= 0) & (local < vocab)
        picked = jnp.take(emb_table, jnp.clip(local, 0, vocab - 1), axis=0)
        picked = jnp.where(owned[:, None], picked, jnp.zeros_like(picked))
        full = picked
        for a in range(1, S):
            full = full + send(picked, [((a, b, c), (0, b, c)) for b in range(T) for c in planes])
        return full, send(full, [((0, b, c), (0, T - 1 - b, c)) for b in range(T) for c in planes])

    blocks = [lax.optimization_barrier((block, ids))[0] for block in blocks]
    early = [relay(c, block) for c, block in zip(rounds[:-1], blocks[:-1])]
    last, early = lax.optimization_barrier((blocks[-1], early))
    received = early + [relay(rounds[-1], last)]
    tok, tok_other = embed(jnp.concatenate([ids[:, seg] for seg in range(segs)]))
    mem_other = send(mem_init, [((0, b, c), (0, T - 1 - b, c)) for b in range(T) for c in planes])

    offset = jnp.arange(turns) - s
    group = offset % S
    segment = jnp.clip(offset // S, 0, segs - 1)
    grouped = lengths.reshape(S, n, segs)
    lens = grouped[group, :, segment]
    active = (offset >= 0) & (offset < segs * S)
    flags = jnp.stack(
        [
            jnp.full((turns,), s == 0),
            (s == 0) & (offset < S),
            jnp.full((turns,), t),
            active & (segment == segs - 1),
        ],
        1,
    ).astype(jnp.int32)
    meta = jnp.concatenate([flags, lens], 1).astype(jnp.int32)

    shifts = [(j, i) for i in range(2) for j in range(T)]
    side = (z == hi).astype(jnp.int32)
    place = jnp.stack([((t + j) % T) * 2 + (side + i) % 2 for j, i in shifts]).astype(jnp.int32)

    smem = pl.BlockSpec(memory_space=pltpu.SMEM)
    vmem = pl.BlockSpec(memory_space=pltpu.VMEM)
    out_proj = w_out[0]
    parts = len(shifts)

    held = pl.pallas_call(
        functools.partial(hold_kernel, len(received)),
        out_shape=[jax.ShapeDtypeStruct(w.shape, w.dtype) for w in received],
        in_specs=[pl.BlockSpec(memory_space=pl.ANY)] * len(received),
        out_specs=[vmem] * len(received),
        scratch_shapes=[pltpu.SemaphoreType.DMA((len(received),))],
        compiler_params=params,
    )(*received)
    weights = [own_block, *held]

    own = jnp.zeros((R, half), jnp.bfloat16)
    other = jnp.zeros((R, half), jnp.bfloat16)
    pools = []
    for k in range(turns):
        step = n * tokens
        at = min(k, segs * S - 1) * step
        tk, tko = tok[at : at + step], tok_other[at : at + step]
        mixed, keep = pl.pallas_call(
            functools.partial(attend_kernel, k, n, tokens, D),
            out_shape=(
                jax.ShapeDtypeStruct((R, cols), jnp.bfloat16),
                jax.ShapeDtypeStruct((R, half), jnp.bfloat16),
            ),
            in_specs=[smem, smem] + [vmem] * (7 + len(weights)),
            out_specs=(vmem, vmem),
            scratch_shapes=[
                pltpu.VMEM((R, 2 * half), jnp.bfloat16),
                pltpu.VMEM((R, 3 * cols), jnp.float32),
            ],
            compiler_params=params,
        )(meta, where, own, other, tk, tko, mem_init, mem_other, norm_gain, *weights)
        shared = [mixed]
        for j, i in shifts[1:]:
            def back(a, b, c):
                return (a, (b - j) % T, planes[(planes.index(c) + i) % 2])

            shared.append(send(mixed, mid(back)))
        pool = k >= (segs - 1) * S
        shapes = [jax.ShapeDtypeStruct((R, half), jnp.bfloat16)]
        if pool:
            shapes.append(jax.ShapeDtypeStruct((n, half), jnp.float32))
        result = pl.pallas_call(
            functools.partial(project_kernel, k, n, tokens, parts, pool),
            out_shape=tuple(shapes),
            in_specs=[smem, smem, smem] + [vmem] * (parts + 2),
            out_specs=tuple([vmem] * len(shapes)),
            compiler_params=params,
        )(meta, place, layer_mix, *shared, keep, out_proj)
        if pool:
            pools.append(result[1])
        if k < turns - 1:
            paired = S % 2 == 0 and k in (0, turns - 2)
            after = [e[0] ^ 1 if paired else (e[0] + 1) % S for e in everyone]
            own = send(result[0], [(e, (a, e[1], e[2])) for e, a in zip(everyone, after)])
            counts = [
                a for a in range(S) if 0 <= k - a < segs * S - (S if a == S - 1 else 0)
            ]
            other = send(
                result[0],
                [
                    (e, (a, T - 1 - e[1] if e[0] in counts else e[1], e[2]))
                    for e, a in zip(everyone, after)
                ],
            )

    mine = lax.dynamic_slice_in_dim(jnp.stack(pools), s, S, 0).reshape(docs, half)
    total = mine
    for a in range(1, S):
        total = total + send(mine, [(e, ((e[0] + a) % S, e[1], e[2])) for e in everyone])
    spread = total
    for k in range(1, D // 2):
        ends = ((lo, lo - k), (hi, hi + k))
        pairs = [((a, b, c), (a, b, e)) for a in range(S) for b in range(T) for c, e in ends]
        got = send(total, pairs + [(e, c) for c, e in pairs])
        spread = jnp.where((z == lo - k) | (z == hi + k), got, spread)
    return spread


def solution(mesh):
    return jax.shard_map(
        body,
        mesh=mesh,
        in_specs=(
            P("doc", None, None),
            P("doc", None),
            P("section", "tp"),
            P(None, "tp"),
            P("section", None),
            P("section", "doc", "tp"),
            P("section", "doc", "tp"),
            P("section", "doc", "tp"),
            P("section", None, "tp"),
            P("section"),
        ),
        out_specs=P(None, "tp"),
        check_vma=False,
    )
```
